256 devices in a mesh: pop: 16 (over x, z_hi, core), tp: 16 (over y, z_lo).
Axes of the slice: x: 4, y: 4, z: 8 (z_hi: 2, z_lo: 4; z = z_hi * 4 + z_lo), core: 2. Of those that a mesh axis runs over, the one named last changes fastest.
Arguments:
- left_factors: bfloat16 [16384, 4096], P(('pop', 'tp')), may hold values from -6 to 6
- right_factors: bfloat16 [16384, 16384], P('pop', 'tp'), may hold values from -6 to 6
- ranks: int32 [16384], P(('pop', 'tp')), may hold values from 0 to 16383, each once
- weight: bfloat16 [4096, 16384], P('pop', 'tp'), may hold values from -3 to 3
Outputs:
- new_weight: bfloat16 [4096, 16384], P(None, 'tp')
The draws below stay inside these ranges and needn't reach their ends.
Inputs may be any that keep to these rules, and one draw needn't show every extreme that they name: ranks holds each of 0 to 16383 exactly once.
All inputs are finite; a program needn't handle non-finite values.
Results may differ from the reference program's by a relative error of at most 0.017.
Values may be sent and summed in bfloat16 or wider, within the bound.
A program may use at most 64 MiB of HBM per device.

```python
import math
import jax
import jax.numpy as jnp
from jax import lax

D = 4096
F = 16384
MEM = 1024
MEMBERS = 16384
N_POP = 16


def block_scale(stream_key, shape, pieces, smallest, largest):
    factor_of = 1.0
    for axis_at, shards_of in pieces:
        heights = jax.random.uniform(jax.random.fold_in(jax.random.fold_in(stream_key, 6), axis_at), (shards_of,), jnp.float32, smallest / len(pieces), largest / len(pieces))
        factor_of = factor_of * jnp.repeat(jnp.exp(heights), shape[axis_at] // shards_of).reshape((-1,) + (1,) * (len(shape) - 1 - axis_at))
    return factor_of


def normal_values(key, dims, spread, most, shards=(), kind=jnp.bfloat16):
    entries = spread * jax.random.normal(key, dims, jnp.float32)
    if shards:
        entries = entries * block_scale(key, dims, shards, -0.22, 0.18)
    return jnp.clip(entries, -most, most).astype(kind)


def setup_inputs(seed: int = 0) -> dict:
    key_list = jax.random.split(jax.random.key(seed), 5)
    return {
        "left_factors": normal_values(key_list[0], (MEMBERS, D), 1.0, 6.0, ((0, 256),)),
        "right_factors": normal_values(key_list[1], (MEMBERS, F), 1.0, 6.0, ((0, 16), (1, 16))),
        "ranks": jax.random.permutation(key_list[2], MEMBERS).astype(jnp.int32),
        "weight": normal_values(key_list[3], (D, F), 0.5, 3.0, ((0, 16), (1, 16))),
    }


def reference(left_factors, right_factors, ranks, weight):
    total = left_factors.shape[0]
    score = (2.0 * ranks.astype(jnp.float32) + 1.0 - total) / total * math.sqrt(3.0 / total)
    scaled = (score[:, None] * left_factors.astype(jnp.float32)).astype(jnp.bfloat16)
    left_groups = scaled.reshape(N_POP, MEM, D)
    right_groups = right_factors.reshape(N_POP, MEM, F)

    def add_group(carry, pair):
        left_part, right_part = pair
        partial_value = jnp.dot(left_part.astype(jnp.float32).T, right_part.astype(jnp.float32), precision=lax.Precision.HIGHEST)
        partial_value = lax.optimization_barrier(partial_value.astype(jnp.bfloat16))
        return (carry + partial_value.astype(jnp.float32), None)
    update, unused = lax.scan(add_group, jnp.zeros((D, F), jnp.float32), (left_groups, right_groups))
    return (weight.astype(jnp.float32) + update).astype(jnp.bfloat16)
```

```python
import functools
import math

import jax
import jax.numpy as jnp
from jax import lax
from jax.experimental import pallas as pl
from jax.experimental.pallas import tpu as pltpu
from jax.sharding import PartitionSpec as P

MESH = pl.DeviceIdType.MESH
X, ZH, CORES, Y, ZL = 4, 2, 2, 4, 4
TP = Y * ZL
CHUNKS = 8
F32, BF16 = jnp.float32, jnp.bfloat16


def kernel(
    total,
    left,
    ranks,
    right,
    weight,
    out,
    halves,
    members,
    lg,
    rall,
    wv,
    part,
    ra,
    rb,
    cl,
    cr,
    zr,
    fin,
    pre_sem,
    z_own_s,
    z_fwd_s,
    z_r,
    y1_s,
    y1_r,
    y2_s,
    y2_r,
    rs1_s,
    rs1_r,
    rs2_s,
    rs2_r,
    z4_s,
    z4_r,
    ag1_s,
    ag1_r,
    ag2_s,
    ag2_r,
    core_s,
    core_r,
    loc_s,
):
    p, t = lax.axis_index("pop"), lax.axis_index("tp")
    x, zh, c = p // 4, (p // 2) % 2, p % 2
    y, zl = t // ZL, t % ZL
    xp, xm, xo = (x + 1) % 4, (x + 3) % 4, (x + 2) % 4
    yp, ym = (y + 1) % 4, (y + 3) % 4
    J = lg.shape[0]
    DR = part.shape[3]

    def dev(x_=x, zh_=zh, c_=c, y_=y, zl_=zl):
        return (x_ * 4 + zh_ * 2 + c_, y_ * ZL + zl_)

    def rcopy(src, dst, ssem, rsem, d):
        return pltpu.make_async_remote_copy(
            src_ref=src, dst_ref=dst, send_sem=ssem, recv_sem=rsem, device_id=d, device_id_type=MESH
        )

    d_xp, d_xm, d_yp, d_ym = dev(x_=xp), dev(x_=xm), dev(y_=yp), dev(y_=ym)
    d_z4, d_c = dev(zh_=1 - zh), dev(c_=1 - c)
    d_zu, d_zd = dev(zl_=jnp.minimum(zl + 1, ZL - 1)), dev(zl_=jnp.maximum(zl - 1, 0))

    r_loc = pltpu.make_async_copy(right, rall.at[:, c], pre_sem.at[0])
    w_loc = pltpu.make_async_copy(weight, wv, pre_sem.at[1])
    r_loc.start()
    w_loc.start()

    bar = pltpu.get_barrier_semaphore()
    for d in (d_xp, d_xm, d_yp, d_ym, d_z4, d_c):
        pl.semaphore_signal(bar, 1, device_id=d, device_id_type=MESH)

    @pl.when(zl < ZL - 1)
    def _():
        pl.semaphore_signal(bar, 1, device_id=d_zu, device_id_type=MESH)

    @pl.when(zl > 0)
    def _():
        pl.semaphore_signal(bar, 1, device_id=d_zd, device_id_type=MESH)

    n_mem = left.shape[0]
    eye = lax.broadcasted_iota(jnp.int32, (n_mem, n_mem), 0) == lax.broadcasted_iota(jnp.int32, (n_mem, n_mem), 1)
    row = (2.0 * ranks[...].astype(F32) + 1.0 - total) / total * math.sqrt(3.0 / total)
    score = jnp.sum(jnp.where(eye, jnp.broadcast_to(row, (n_mem, n_mem)), 0.0), axis=1, keepdims=True)
    for m in range(8):
        for h in range(2):
            lo = 256 * (2 * m + h)
            halves[h, :, 256 * m : 256 * m + 256] = (score * left[:, lo : lo + 256].astype(F32)).astype(BF16)

    pl.semaphore_wait(bar, 6 + (zl < ZL - 1).astype(jnp.int32) + (zl > 0).astype(jnp.int32))

    m_rem = rcopy(halves.at[1 - c], members.at[c], pre_sem.at[2], pre_sem.at[3], d_c)
    m_rem.start()
    r_rem = rcopy(right, rall.at[:, c], pre_sem.at[4], pre_sem.at[5], d_c)
    r_rem.start()
    members[c] = halves[c]
    m_rem.wait_recv()

    for m in range(8):
        both = members[:, :, 256 * m : 256 * m + 256].reshape(2 * n_mem, 256)
        cols = both.astype(F32).T.astype(BF16)
        for j in range(J):
            lg[j, t, m * DR : (m + 1) * DR, :] = cols[j * DR : (j + 1) * DR]

    def z_own(j, up):
        ref = lg.at[j, t]
        return rcopy(ref, ref, z_own_s.at[j, up], z_r.at[j, zl], d_zu if up else d_zd)

    def z_fwd(j, s, up):
        ref = lg.at[j, y * ZL + s]
        return rcopy(ref, ref, z_fwd_s.at[j, s], z_r.at[j, s], d_zu if up else d_zd)

    def y1(j, s, plus):
        ref = lg.at[j, y * ZL + s]
        return rcopy(ref, ref, y1_s.at[j, plus, s], y1_r.at[j, plus, s], d_yp if plus else d_ym)

    def y1_in(j, s, plus):
        ref = lg.at[j, (ym if plus else yp) * ZL + s]
        return rcopy(ref, ref, y1_s.at[j, plus, s], y1_r.at[j, plus, s], d_yp if plus else d_ym)

    def y2(j, plus):
        b = ym * ZL if plus else yp * ZL + ZL // 2
        ref = lg.at[j, pl.ds(b, ZL // 2)]
        return rcopy(ref, ref, y2_s.at[j, plus], y2_r.at[j, plus], d_yp if plus else d_ym)

    def rs1(j, plus):
        if plus:
            return rcopy(part.at[j, xo, 0], ra.at[j], rs1_s.at[j, 1], rs1_r.at[j, 1], d_xp)
        return rcopy(part.at[j, xo, 1], rb.at[j], rs1_s.at[j, 0], rs1_r.at[j, 0], d_xm)

    def rs2(j, plus):
        if plus:
            return rcopy(part.at[j, xp], cl.at[j], rs2_s.at[j, 1], rs2_r.at[j, 1], d_xp)
        return rcopy(part.at[j, xm], cr.at[j], rs2_s.at[j, 0], rs2_r.at[j, 0], d_xm)

    def z4(j):
        return rcopy(part.at[j, x], zr.at[j], z4_s.at[j], z4_r.at[j], d_z4)

    def ag1(j, plus):
        return rcopy(fin.at[j], out.at[x, :, c, j], ag1_s.at[j, plus], ag1_r.at[j, plus], d_xp if plus else d_xm)

    def ag2(j, plus):
        ref = out.at[xm, 0, c, j] if plus else out.at[xp, 1, c, j]
        return rcopy(ref, ref, ag2_s.at[j, plus], ag2_r.at[j, plus], d_xp if plus else d_xm)

    def core(j, k):
        b = (x + k) % 4
        dst = out.at[b, :, c, j]
        return rcopy(fin.at[j] if k == 0 else dst, dst, core_s.at[j, k], core_r.at[j, k], d_c)

    def loc(j):
        return pltpu.make_async_copy(fin.at[j], out.at[x, :, c, j], loc_s.at[j])

    def st_own(j):
        @pl.when(zl < ZL - 1)
        def _():
            z_own(j, 1).start()

        @pl.when(zl > 0)
        def _():
            z_own(j, 0).start()

        y1(j, zl, 1).start()
        y1(j, zl, 0).start()

    def st_z(k, j):
        for up in (1, 0):
            s = zl - k if up else zl + k
            there = (s >= 0) if up else (s < ZL)
            on = (zl < ZL - 1) if up else (zl > 0)

            @pl.when(there)
            def _():
                z_fwd(j, s, up).wait_recv()

                @pl.when(on)
                def _():
                    z_fwd(j, s, up).start()

                y1(j, s, 1).start()
                y1(j, s, 0).start()

    def st_y2(j):
        for s in range(ZL):
            y1_in(j, s, 1).wait_recv()
        y2(j, 1).start()
        for s in range(ZL):
            y1_in(j, s, 0).wait_recv()
        y2(j, 0).start()

    def st_gemm(j):
        y2(j, 1).wait_recv()
        y2(j, 0).wait_recv()
        lhs = jnp.concatenate([lg[j, s] for s in range(TP)], axis=1)
        for n in range(4):
            rhs = rall[:, :, :, 256 * n : 256 * n + 256].reshape(TP * 2 * n_mem, 256)
            acc = jnp.dot(lhs, rhs, preferred_element_type=F32)
            part[j, :, :, :, 256 * n : 256 * n + 256] = acc.astype(BF16).reshape(X, ZH, DR, 256)
        rs1(j, 1).start()
        rs1(j, 0).start()

    def st_rs2(j):
        rs1(j, 1).wait_recv()
        part[j, xp, 0] = (part[j, xp, 0].astype(F32) + ra[j].astype(F32)).astype(BF16)
        rs2(j, 1).start()
        rs1(j, 0).wait_recv()
        part[j, xm, 1] = (part[j, xm, 1].astype(F32) + rb[j].astype(F32)).astype(BF16)
        rs2(j, 0).start()

    def st_sum(j):
        rs2(j, 1).wait_recv()
        rs2(j, 0).wait_recv()
        w = wv[j].astype(F32)
        for h in range(ZH):
            mine = part[j, x, h].astype(F32) + jnp.where(zh == h, w, 0.0)
            part[j, x, h] = (mine + cl[j, h].astype(F32) + cr[j, h].astype(F32)).astype(BF16)
        z4(j).start()

    def st_fin(j):
        z4(j).wait_recv()
        fin[j] = (part[j, x].astype(F32) + zr[j].astype(F32)).astype(BF16)
        ag1(j, 1).start()
        ag1(j, 0).start()
        core(j, 0).start()
        loc(j).start()

    def st_ag2(j):
        ag1(j, 1).wait_recv()
        ag2(j, 1).start()
        core(j, 3).start()
        ag1(j, 0).wait_recv()
        ag2(j, 0).start()
        core(j, 1).start()

    def st_last(j):
        ag2(j, 1).wait_recv()
        ag2(j, 0).wait_recv()
        core(j, 2).start()

    stages = [
        (st_last, 10),
        (st_ag2, 9),
        (st_fin, 8),
        (st_sum, 6),
        (st_rs2, 5),
        (st_gemm, 4),
        (st_y2, 3),
        (functools.partial(st_z, 3), 2),
        (functools.partial(st_z, 2), 1),
        (functools.partial(st_z, 1), 0),
    ]

    st_own(0)

    def body(i, carry):
        for fn, skew in stages:
            j = i - skew

            @pl.when(jnp.logical_and(j >= 0, j < J))
            def _():
                if fn is st_gemm:

                    @pl.when(j == 0)
                    def _():
                        r_loc.wait()
                        w_loc.wait()
                        r_rem.wait_recv()

                fn(j)

        @pl.when(i + 1 < J)
        def _():
            st_own(i + 1)

        return carry

    lax.fori_loop(0, J + 10, body, 0)

    m_rem.wait_send()
    r_rem.wait_send()

    def drain(j, carry):
        for k in range(4):
            core(j, k).wait_recv()
            core(j, k).wait_send()
        for plus in (0, 1):
            for s in range(ZL):
                y1(j, s, plus).wait_send()
            y2(j, plus).wait_send()
            rs1(j, plus).wait_send()
            rs2(j, plus).wait_send()
            ag1(j, plus).wait_send()
            ag2(j, plus).wait_send()
        z4(j).wait_send()
        loc(j).wait()

        @pl.when(zl < ZL - 1)
        def _():
            z_own(j, 1).wait_send()
            for s in range(ZL - 2):

                @pl.when(s < zl)
                def _():
                    z_fwd(j, s, 1).wait_send()

        @pl.when(zl > 0)
        def _():
            z_own(j, 0).wait_send()
            for s in range(2, ZL):

                @pl.when(s > zl)
                def _():
                    z_fwd(j, s, 0).wait_send()

        return carry

    lax.fori_loop(0, J, drain, 0)


def per_device(left_factors, right_factors, ranks, weight):
    n_mem, width = left_factors.shape
    members, cols = right_factors.shape
    total = members * lax.axis_size("pop")
    J = CHUNKS
    DR = weight.shape[0] // J
    dma = pltpu.SemaphoreType.DMA
    anyspace = pl.BlockSpec(memory_space=pl.ANY)
    vmem = pl.BlockSpec(memory_space=pltpu.VMEM)
    out = pl.pallas_call(
        functools.partial(kernel, total),
        out_shape=jax.ShapeDtypeStruct((X, ZH, CORES, J, DR, cols), BF16),
        in_specs=[vmem, vmem, anyspace, anyspace],
        out_specs=anyspace,
        scratch_shapes=[
            pltpu.VMEM((2, n_mem, width // 2), BF16),
            pltpu.VMEM((2, n_mem, width // 2), BF16),
            pltpu.VMEM((J, TP, 8 * DR, 2 * n_mem), BF16),
            pltpu.VMEM((TP, 2, n_mem, cols), BF16),
            pltpu.VMEM((J, DR, cols), BF16),
            pltpu.VMEM((J, X, ZH, DR, cols), BF16),
            pltpu.VMEM((J, DR, cols), BF16),
            pltpu.VMEM((J, DR, cols), BF16),
            pltpu.VMEM((J, ZH, DR, cols), BF16),
            pltpu.VMEM((J, ZH, DR, cols), BF16),
            pltpu.VMEM((J, ZH, DR, cols), BF16),
            pltpu.VMEM((J, ZH, DR, cols), BF16),
            dma((6,)),
            dma((J, 2)),
            dma((J, ZL)),
            dma((J, ZL)),
            dma((J, 2, ZL)),
            dma((J, 2, ZL)),
            dma((J, 2)),
            dma((J, 2)),
            dma((J, 2)),
            dma((J, 2)),
            dma((J, 2)),
            dma((J, 2)),
            dma((J,)),
            dma((J,)),
            dma((J, 2)),
            dma((J, 2)),
            dma((J, 2)),
            dma((J, 2)),
            dma((J, 4)),
            dma((J, 4)),
            dma((J,)),
        ],
        compiler_params=pltpu.CompilerParams(
            collective_id=0, has_side_effects=True, vmem_limit_bytes=48 * 2**20
        ),
    )(
        left_factors,
        ranks.reshape(1, n_mem),
        right_factors.reshape(TP, n_mem, cols),
        weight.reshape(J, DR, cols),
    )
    return out.reshape(X * ZH * CORES * J * DR, cols)


def solution(mesh):
    return jax.shard_map(
        per_device,
        mesh=mesh,
        in_specs=(P(("pop", "tp"), None), P("pop", "tp"), P(("pop", "tp")), P("pop", "tp")),
        out_specs=P(None, "tp"),
        check_vma=False,
    )
```

```python
import functools
import math

import jax
import jax.numpy as jnp
from jax import lax
from jax.experimental import pallas as pl
from jax.experimental.pallas import tpu as pltpu
from jax.sharding import PartitionSpec as P

MESH = pl.DeviceIdType.MESH
X, ZH, CORES, Y, ZL = 4, 2, 2, 4, 4
TP = Y * ZL
CHUNKS = 16
STEPS = 7
ORDER = (
    0x1100000, 0x2222111, 0x3333032, 0x0041404, 0x5125144, 0x3356102, 0x5712062, 0x4435763,
    0x8671600, 0x1281244, 0x9293557, 0x5608703, 0x4804356, 0x8469712, 0x9572163, 0x3782915,
    0x7362546, 0x5367948, 0x6945784, 0x6759657, 0xA867AA8, 0x7A9887A, 0x888989A, 0xAAA9999,
    0xAAAA9AA, 0xFFFFFFA,
)
F32, BF16 = jnp.float32, jnp.bfloat16


def kernel(
    total,
    left_in,
    ranks_in,
    right,
    weight,
    out,
    left,
    ranks,
    halves,
    members,
    lg,
    rall,
    wv,
    part,
    rh,
    rf,
    zr,
    pre_sem,
    z_s,
    z_r,
    y_s,
    y1_r,
    y2_r,
    rs_s,
    rs1_r,
    rs2_r,
    z4_s,
    z4_r,
    ag_s,
    ag1_r,
    ag2_r,
    core_s,
    core_r,
):
    p, t = lax.axis_index("pop"), lax.axis_index("tp")
    x, zh, c = p // 4, (p // 2) % 2, p % 2
    y, zl = t // ZL, t % ZL
    xp, xm, xo = (x + 1) % 4, (x + 3) % 4, (x + 2) % 4
    yp, ym = (y + 1) % 4, (y + 3) % 4
    J = lg.shape[0]
    DR = part.shape[3]

    def dev(x_=x, zh_=zh, c_=c, y_=y, zl_=zl):
        return (x_ * 4 + zh_ * 2 + c_, y_ * ZL + zl_)

    def rcopy(src, dst, ssem, rsem, d):
        return pltpu.make_async_remote_copy(
            src_ref=src, dst_ref=dst, send_sem=ssem, recv_sem=rsem, device_id=d, device_id_type=MESH
        )

    d_xp, d_xm, d_yp, d_ym = dev(x_=xp), dev(x_=xm), dev(y_=yp), dev(y_=ym)
    d_z4, d_c = dev(zh_=1 - zh), dev(c_=1 - c)
    d_zu, d_zd = dev(zl_=jnp.minimum(zl + 1, ZL - 1)), dev(zl_=jnp.maximum(zl - 1, 0))

    r_loc = pltpu.make_async_copy(right, rall.at[:, c], pre_sem.at[0])
    w_loc = pltpu.make_async_copy(weight, wv, pre_sem.at[1])
    left_loc = pltpu.make_async_copy(left_in, left, pre_sem.at[6])
    ranks_loc = pltpu.make_async_copy(ranks_in, ranks, pre_sem.at[7])
    ranks_loc.start()
    left_loc.start()
    r_loc.start()
    w_loc.start()

    bar = pltpu.get_barrier_semaphore()
    for d in (d_xp, d_xm, d_yp, d_ym, d_z4, d_c):
        pl.semaphore_signal(bar, 1, device_id=d, device_id_type=MESH)

    @pl.when(zl < ZL - 1)
    def _():
        pl.semaphore_signal(bar, 1, device_id=d_zu, device_id_type=MESH)

    @pl.when(zl > 0)
    def _():
        pl.semaphore_signal(bar, 1, device_id=d_zd, device_id_type=MESH)

    n_mem = left.shape[0]
    eye = lax.broadcasted_iota(jnp.int32, (n_mem, n_mem), 0) == lax.broadcasted_iota(jnp.int32, (n_mem, n_mem), 1)
    ranks_loc.wait()
    left_loc.wait()
    row = (2.0 * ranks[...].astype(F32) + 1.0 - total) / total * math.sqrt(3.0 / total)
    score = jnp.sum(jnp.where(eye, jnp.broadcast_to(row, (n_mem, n_mem)), 0.0), axis=1, keepdims=True)
    for m in range(8):
        for h in range(2):
            lo = 256 * (2 * m + h)
            halves[h, :, 256 * m : 256 * m + 256] = (score * left[:, lo : lo + 256].astype(F32)).astype(BF16)

    pl.semaphore_wait(bar, 6 + (zl < ZL - 1).astype(jnp.int32) + (zl > 0).astype(jnp.int32))

    m_rem = rcopy(halves.at[1 - c], members.at[c], pre_sem.at[2], pre_sem.at[3], d_c)
    m_rem.start()
    r_rem = rcopy(right, rall.at[:, c], pre_sem.at[4], pre_sem.at[5], d_c)
    r_rem.start()
    members[c] = halves[c]
    m_rem.wait_recv()

    for m in range(8):
        both = members[:, :, 256 * m : 256 * m + 256].reshape(2 * n_mem, 256)
        cols = both.astype(F32).T.astype(BF16)
        for j in range(J):
            lg[j, t, m * DR : (m + 1) * DR, :] = cols[j * DR : (j + 1) * DR]

    def z_own(j, up):
        ref = lg.at[j, t]
        return rcopy(ref, ref, z_s.at[j], z_r.at[j, zl], d_zu if up else d_zd)

    def z_fwd(j, s, up):
        ref = lg.at[j, y * ZL + s]
        return rcopy(ref, ref, z_s.at[j], z_r.at[j, s], d_zu if up else d_zd)

    def y1(j, s, plus):
        ref = lg.at[j, y * ZL + s]
        return rcopy(ref, ref, y_s.at[j], y1_r.at[j, plus], d_yp if plus else d_ym)

    def y1_in(j, plus):
        ref = lg.at[j, pl.ds((ym if plus else yp) * ZL, ZL)]
        return rcopy(ref, ref, y_s.at[j], y1_r.at[j, plus], d_yp if plus else d_ym)

    def y2(j, plus):
        b = ym * ZL if plus else yp * ZL + ZL // 2
        ref = lg.at[j, pl.ds(b, ZL // 2)]
        return rcopy(ref, ref, y_s.at[j], y2_r.at[j], d_yp if plus else d_ym)

    def y2_in(j):
        ref = lg.at[j, pl.ds(((y + 2) % 4) * ZL, ZL)]
        return rcopy(ref, ref, y_s.at[j], y2_r.at[j], d_yp)

    def rs1(j, plus):
        if plus:
            return rcopy(part.at[j, xo, 0], rh.at[j, 1], rs_s.at[j], rs1_r.at[j, 1], d_xp)
        return rcopy(part.at[j, xo, 1], rh.at[j, 0], rs_s.at[j], rs1_r.at[j, 0], d_xm)

    def rs2(j, plus):
        if plus:
            return rcopy(part.at[j, xp], rf.at[j, 1], rs_s.at[j], rs2_r.at[j], d_xp)
        return rcopy(part.at[j, xm], rf.at[j, 0], rs_s.at[j], rs2_r.at[j], d_xm)

    def rs2_in(j):
        return rcopy(rf.at[j], rf.at[j], rs_s.at[j], rs2_r.at[j], d_xp)

    def z4(j):
        return rcopy(part.at[j, x], zr.at[j], z4_s.at[j], z4_r.at[j], d_z4)

    def ag1(j, plus):
        ref = out.at[x, :, c, j]
        return rcopy(ref, ref, ag_s.at[j], ag1_r.at[j, plus], d_xp if plus else d_xm)

    def ag2(j, plus):
        ref = out.at[xm, 0, c, j] if plus else out.at[xp, 1, c, j]
        return rcopy(ref, ref, ag_s.at[j], ag2_r.at[j], d_xp if plus else d_xm)

    def ag2_in(j):
        ref = out.at[xo, :, c, j]
        return rcopy(ref, ref, ag_s.at[j], ag2_r.at[j], d_xp)

    def core(j, k):
        ref = out.at[(x + k) % 4, :, c, j]
        return rcopy(ref, ref, core_s.at[j], core_r.at[j], d_c)

    def drain_left(j):
        sent = lg.at[j, pl.ds(0, 3 * ZL)]
        rcopy(sent, sent, y_s.at[j], y2_r.at[j], d_yp).wait_send()
        edge = jnp.logical_or(zl == 0, zl == ZL - 1)
        for n, here in ((1, edge), (5, jnp.logical_not(edge))):

            @pl.when(here)
            def _():
                some = lg.at[j, pl.ds(0, n)]
                rcopy(some, some, z_s.at[j], z_r.at[j, 0], d_c).wait_send()

    def drain_sums(j):
        sent = part.at[j, pl.ds(0, 3)]
        rcopy(sent, sent, rs_s.at[j], rs2_r.at[j], d_xp).wait_send()

    def drain_out(j):
        sent = out.at[pl.ds(0, 3), :, c, j]
        rcopy(sent, sent, ag_s.at[j], ag2_r.at[j], d_xp).wait_send()
        z4(j).wait_send()
        sent = out.at[:, :, c, j]
        rcopy(sent, sent, core_s.at[j], core_r.at[j], d_c).wait_send()
        came = out.at[:, :, 1 - c, j]
        rcopy(came, came, core_s.at[j], core_r.at[j], d_c).wait_recv()

    def st_own(j):
        @pl.when(zl < ZL - 1)
        def _():
            z_own(j, 1).start()

        @pl.when(zl > 0)
        def _():
            z_own(j, 0).start()

        y1(j, zl, 1).start()
        y1(j, zl, 0).start()

    def st_z(k, j):
        for up in (1, 0):
            s = zl - k if up else zl + k
            there = (s >= 0) if up else (s < ZL)
            on = (zl < ZL - 1) if up else (zl > 0)

            @pl.when(there)
            def _():
                z_fwd(j, s, up).wait_recv()

                @pl.when(on)
                def _():
                    z_fwd(j, s, up).start()

                y1(j, s, 1).start()
                y1(j, s, 0).start()

    def st_y2(j):
        y1_in(j, 1).wait_recv()
        y2(j, 1).start()
        y1_in(j, 0).wait_recv()
        y2(j, 0).start()

    def st_gemm(j):
        @pl.when(j == 0)
        def _():
            r_loc.wait()
            w_loc.wait()
            r_rem.wait_recv()

        y2_in(j).wait_recv()
        lhs = jnp.concatenate([lg[j, s] for s in range(TP)], axis=1)
        for n in range(4):
            rhs = rall[:, :, :, 256 * n : 256 * n + 256].reshape(TP * 2 * n_mem, 256)
            acc = jnp.dot(lhs, rhs, preferred_element_type=F32)
            part[j, :, :, :, 256 * n : 256 * n + 256] = acc.astype(BF16).reshape(X, ZH, DR, 256)
        rs1(j, 1).start()
        rs1(j, 0).start()

    def st_rs2(j):
        rs1(j, 1).wait_recv()
        part[j, xp, 0] = (part[j, xp, 0].astype(F32) + rh[j, 1].astype(F32)).astype(BF16)
        rs2(j, 1).start()
        rs1(j, 0).wait_recv()
        part[j, xm, 1] = (part[j, xm, 1].astype(F32) + rh[j, 0].astype(F32)).astype(BF16)
        rs2(j, 0).start()

    def st_sum(j):
        rs2_in(j).wait_recv()
        w = wv[j].astype(F32)
        for h in range(ZH):
            mine = part[j, x, h].astype(F32) + jnp.where(zh == h, w, 0.0)
            part[j, x, h] = (mine + rf[j, 1, h].astype(F32) + rf[j, 0, h].astype(F32)).astype(BF16)
        z4(j).start()
        drain_left(j)

    def st_fin(j):
        z4(j).wait_recv()
        for h in range(ZH):
            out[x, h, c, j] = (part[j, x, h].astype(F32) + zr[j, h].astype(F32)).astype(BF16)
        ag1(j, 1).start()
        ag1(j, 0).start()
        core(j, 0).start()
        drain_sums(j)

    def st_ag2(j):
        ag1(j, 1).wait_recv()
        ag2(j, 1).start()
        core(j, 3).start()
        ag1(j, 0).wait_recv()
        ag2(j, 0).start()
        core(j, 1).start()

    def st_last(j):
        ag2_in(j).wait_recv()
        core(j, 2).start()

        @pl.when(j >= 2)
        def _():
            drain_out(j - 2)

    stages = (
        st_own,
        functools.partial(st_z, 1),
        functools.partial(st_z, 2),
        functools.partial(st_z, 3),
        st_y2,
        st_gemm,
        st_rs2,
        st_sum,
        st_fin,
        st_ag2,
        st_last,
    )

    def step(i, carry):
        word, counts = carry[0], carry[1:]
        now = lax.rem(word, 16)
        for n, fn in enumerate(stages):

            @pl.when(now == n)
            def _():
                fn(counts[n])

        return (lax.div(word, 16),) + tuple(
            jnp.where(now == n, count + 1, count) for n, count in enumerate(counts)
        )

    def group(g, counts):
        word = jnp.int32(ORDER[0])
        for k, w in enumerate(ORDER):
            word = jnp.where(g == k, jnp.int32(w), word)
        return lax.fori_loop(0, STEPS, step, (word,) + counts)[1:]

    lax.fori_loop(0, len(ORDER), group, (jnp.int32(0),) * len(stages))
    m_rem.wait_send()
    r_rem.wait_send()
    drain_out(J - 2)
    drain_out(J - 1)


def per_device(left_factors, right_factors, ranks, weight):
    n_mem, width = left_factors.shape
    members, cols = right_factors.shape
    total = members * lax.axis_size("pop")
    J = CHUNKS
    DR = weight.shape[0] // J
    dma = pltpu.SemaphoreType.DMA
    anyspace = pl.BlockSpec(memory_space=pl.ANY)
    vmem = pl.BlockSpec(memory_space=pltpu.VMEM)
    out = pl.pallas_call(
        functools.partial(kernel, total),
        out_shape=pltpu.VMEM((X, ZH, CORES, J, DR, cols), BF16),
        in_specs=[anyspace] * 4,
        out_specs=vmem,
        scratch_shapes=[
            pltpu.VMEM((n_mem, width), BF16),
            pltpu.VMEM((1, n_mem), jnp.int32),
            pltpu.VMEM((2, n_mem, width // 2), BF16),
            pltpu.VMEM((2, n_mem, width // 2), BF16),
            pltpu.VMEM((J, TP, 8 * DR, 2 * n_mem), BF16),
            pltpu.VMEM((TP, 2, n_mem, cols), BF16),
            pltpu.VMEM((J, DR, cols), BF16),
            pltpu.VMEM((J, X, ZH, DR, cols), BF16),
            pltpu.VMEM((J, 2, DR, cols), BF16),
            pltpu.VMEM((J, 2, ZH, DR, cols), BF16),
            pltpu.VMEM((J, ZH, DR, cols), BF16),
            dma((8,)),
            dma((J,)),
            dma((J, ZL)),
            dma((J,)),
            dma((J, 2)),
            dma((J,)),
            dma((J,)),
            dma((J, 2)),
            dma((J,)),
            dma((J,)),
            dma((J,)),
            dma((J,)),
            dma((J, 2)),
            dma((J,)),
            dma((J,)),
            dma((J,)),
        ],
        compiler_params=pltpu.CompilerParams(
            collective_id=0, has_side_effects=True, vmem_limit_bytes=48 * 2**20
        ),
    )(
        left_factors,
        ranks.reshape(1, n_mem),
        right_factors.reshape(TP, n_mem, cols),
        weight.reshape(J, DR, cols),
    )
    return out.reshape(X * ZH * CORES * J * DR, cols)


def solution(mesh):
    return jax.shard_map(
        per_device,
        mesh=mesh,
        in_specs=(P(("pop", "tp"), None), P("pop", "tp"), P(("pop", "tp")), P("pop", "tp")),
        out_specs=P(None, "tp"),
        check_vma=False,
    )
```

```python
import functools
import math

import jax
import jax.numpy as jnp
from jax import lax
from jax.experimental import pallas as pl
from jax.experimental.pallas import tpu as pltpu
from jax.sharding import PartitionSpec as P

MESH = pl.DeviceIdType.MESH
X, ZH, CORES, Y, ZL = 4, 2, 2, 4, 4
TP = Y * ZL
CHUNKS = 16
STEPS = 7
ORDER = (
    0x1110110, 0x2111100, 0x1211102, 0x0230033, 0x0450454, 0x3062025, 0x3254603, 0x0726224,
    0x4672350, 0x3427853, 0x5436283, 0x2568497, 0x5608379, 0x2837944, 0x538756A, 0x87B99A6,
    0x624A546, 0x4A7589B, 0x63BA357, 0xB679181, 0x958944A, 0xA75876B, 0x97896C1, 0xB7CCA68,
    0xA8B9789, 0x9ABAC89, 0xCCABB9A, 0xBCAABAC, 0xBBCCBCB, 0xFFCCCCC,
)
F32, BF16 = jnp.float32, jnp.bfloat16


def kernel(
    total,
    left_in,
    ranks_in,
    right,
    weight,
    out,
    ranks,
    members,
    lg,
    rall,
    wv,
    part,
    rh,
    rf,
    zr,
    pre_sem,
    z_s,
    z_r,
    y_s,
    y1_r,
    y2_r,
    rs_s,
    rs1_r,
    rs2_r,
    z4_s,
    z4_r,
    ag_s,
    ag1_r,
    ag2_r,
    core_s,
    core_r,
):
    p, t = lax.axis_index("pop"), lax.axis_index("tp")
    x, zh, c = p // 4, (p // 2) % 2, p % 2
    y, zl = t // ZL, t % ZL
    xp, xm, xo = (x + 1) % 4, (x + 3) % 4, (x + 2) % 4
    yp, ym = (y + 1) % 4, (y + 3) % 4
    J = lg.shape[0]
    DR = part.shape[3]

    def dev(x_=x, zh_=zh, c_=c, y_=y, zl_=zl):
        return (x_ * 4 + zh_ * 2 + c_, y_ * ZL + zl_)

    def rcopy(src, dst, ssem, rsem, d):
        return pltpu.make_async_remote_copy(
            src_ref=src, dst_ref=dst, send_sem=ssem, recv_sem=rsem, device_id=d, device_id_type=MESH
        )

    d_xp, d_xm, d_yp, d_ym = dev(x_=xp), dev(x_=xm), dev(y_=yp), dev(y_=ym)
    d_z4, d_c = dev(zh_=1 - zh), dev(c_=1 - c)
    d_zu, d_zd = dev(zl_=jnp.minimum(zl + 1, ZL - 1)), dev(zl_=jnp.maximum(zl - 1, 0))

    r_loc = pltpu.make_async_copy(right, rall.at[:, c], pre_sem.at[0])
    w_loc = pltpu.make_async_copy(weight, wv, pre_sem.at[1])
    ranks_loc = pltpu.make_async_copy(ranks_in, ranks.at[c], pre_sem.at[2])
    ranks_loc.start()

    def left_block(m, half):
        return left_in.at[:, pl.ds(pl.multiple_of(256 * (2 * m + half), 256), 256)]

    for m in range(8):
        pltpu.make_async_copy(left_block(m, c), members.at[c, :, pl.ds(256 * m, 256)], pre_sem.at[3]).start()
    r_loc.start()
    w_loc.start()

    bar = pltpu.get_barrier_semaphore()
    for d in (d_xp, d_xm, d_yp, d_ym, d_z4, d_c):
        pl.semaphore_signal(bar, 1, device_id=d, device_id_type=MESH)

    @pl.when(zl < ZL - 1)
    def _():
        pl.semaphore_signal(bar, 1, device_id=d_zu, device_id_type=MESH)

    @pl.when(zl > 0)
    def _():
        pl.semaphore_signal(bar, 1, device_id=d_zd, device_id_type=MESH)

    pl.semaphore_wait(bar, 6 + (zl < ZL - 1).astype(jnp.int32) + (zl > 0).astype(jnp.int32))

    ranks_rem = rcopy(ranks_in, ranks.at[c], pre_sem.at[6], pre_sem.at[7], d_c)
    ranks_rem.start()
    for m in range(8):
        rcopy(left_block(m, 1 - c), members.at[c, :, pl.ds(256 * m, 256)], pre_sem.at[8], pre_sem.at[9], d_c).start()
    r_rem = rcopy(right, rall.at[:, c], pre_sem.at[4], pre_sem.at[5], d_c)
    r_rem.start()

    n_mem = left_in.shape[0]
    m_rem = rcopy(members.at[c], members.at[c], pre_sem.at[8], pre_sem.at[9], d_c)
    ranks_loc.wait()
    ranks_rem.wait_recv()
    eye = lax.broadcasted_iota(jnp.int32, (n_mem, n_mem), 0) == lax.broadcasted_iota(jnp.int32, (n_mem, n_mem), 1)
    scores = []
    for k in range(CORES):
        row = (2.0 * ranks[k].astype(F32) + 1.0 - total) / total * math.sqrt(3.0 / total)
        row = jnp.where(eye, jnp.broadcast_to(row, (n_mem, n_mem)), 0.0)
        scores.append(jnp.sum(row, axis=1, keepdims=True))
    score = jnp.concatenate(scores, axis=0)
    pltpu.make_async_copy(members.at[c], members.at[c], pre_sem.at[3]).wait()
    m_rem.wait_recv()
    for m in range(8):
        both = members[:, :, 256 * m : 256 * m + 256].reshape(2 * n_mem, 256).astype(F32)
        cols = (score * both).astype(BF16).astype(F32).T.astype(BF16)
        for j in range(J):
            lg[j, t, m * DR : (m + 1) * DR, :] = cols[j * DR : (j + 1) * DR]

    def z_own(j, up):
        ref = lg.at[j, t]
        return rcopy(ref, ref, z_s.at[j], z_r.at[j, zl], d_zu if up else d_zd)

    def z_fwd(j, s, up):
        ref = lg.at[j, y * ZL + s]
        return rcopy(ref, ref, z_s.at[j], z_r.at[j, s], d_zu if up else d_zd)

    def y1(j, s, plus):
        ref = lg.at[j, y * ZL + s]
        return rcopy(ref, ref, y_s.at[j], y1_r.at[j, plus], d_yp if plus else d_ym)

    def y1_in(j, plus):
        ref = lg.at[j, pl.ds((ym if plus else yp) * ZL, ZL)]
        return rcopy(ref, ref, y_s.at[j], y1_r.at[j, plus], d_yp if plus else d_ym)

    def y2(j, plus):
        b = ym * ZL if plus else yp * ZL + ZL // 2
        ref = lg.at[j, pl.ds(b, ZL // 2)]
        return rcopy(ref, ref, y_s.at[j], y2_r.at[j], d_yp if plus else d_ym)

    def y2_in(j):
        ref = lg.at[j, pl.ds(((y + 2) % 4) * ZL, ZL)]
        return rcopy(ref, ref, y_s.at[j], y2_r.at[j], d_yp)

    def rs1(j, plus):
        if plus:
            return rcopy(part.at[j, xo, 0], rh.at[j, 1], rs_s.at[j], rs1_r.at[j, 1], d_xp)
        return rcopy(part.at[j, xo, 1], rh.at[j, 0], rs_s.at[j], rs1_r.at[j, 0], d_xm)

    def rs2(j, plus):
        if plus:
            return rcopy(part.at[j, xp], rf.at[j, 1], rs_s.at[j], rs2_r.at[j], d_xp)
        return rcopy(part.at[j, xm], rf.at[j, 0], rs_s.at[j], rs2_r.at[j], d_xm)

    def rs2_in(j):
        return rcopy(rf.at[j], rf.at[j], rs_s.at[j], rs2_r.at[j], d_xp)

    def z4(j):
        return rcopy(part.at[j, x], zr.at[j], z4_s.at[j], z4_r.at[j], d_z4)

    def ag1(j, plus):
        ref = out.at[x, :, c, j]
        return rcopy(ref, ref, ag_s.at[j], ag1_r.at[j, plus], d_xp if plus else d_xm)

    def ag2(j, plus):
        ref = out.at[xm, 0, c, j] if plus else out.at[xp, 1, c, j]
        return rcopy(ref, ref, ag_s.at[j], ag2_r.at[j], d_xp if plus else d_xm)

    def ag2_in(j):
        ref = out.at[xo, :, c, j]
        return rcopy(ref, ref, ag_s.at[j], ag2_r.at[j], d_xp)

    def core(j, k):
        ref = out.at[(x + k) % 4, :, c, j]
        return rcopy(ref, ref, core_s.at[j], core_r.at[j], d_c)

    def drain_left(j):
        sent = lg.at[j, pl.ds(0, 3 * ZL)]
        rcopy(sent, sent, y_s.at[j], y2_r.at[j], d_yp).wait_send()
        edge = jnp.logical_or(zl == 0, zl == ZL - 1)
        for n, here in ((1, edge), (5, jnp.logical_not(edge))):

            @pl.when(here)
            def _():
                some = lg.at[j, pl.ds(0, n)]
                rcopy(some, some, z_s.at[j], z_r.at[j, 0], d_c).wait_send()

    def drain_sums(j):
        sent = part.at[j, pl.ds(0, 3)]
        rcopy(sent, sent, rs_s.at[j], rs2_r.at[j], d_xp).wait_send()

    def drain_out(j):
        sent = out.at[pl.ds(0, 3), :, c, j]
        rcopy(sent, sent, ag_s.at[j], ag2_r.at[j], d_xp).wait_send()
        z4(j).wait_send()
        sent = out.at[:, :, c, j]
        rcopy(sent, sent, core_s.at[j], core_r.at[j], d_c).wait_send()
        came = out.at[:, :, 1 - c, j]
        rcopy(came, came, core_s.at[j], core_r.at[j], d_c).wait_recv()

    def st_own_z(j):
        @pl.when(zl < ZL - 1)
        def _():
            z_own(j, 1).start()

        @pl.when(zl > 0)
        def _():
            z_own(j, 0).start()

    def st_own_y(j):
        y1(j, zl, 1).start()
        y1(j, zl, 0).start()

    def st_z(k, j):
        for up in (1, 0):
            s = zl - k if up else zl + k
            there = (s >= 0) if up else (s < ZL)
            on = (zl < ZL - 1) if up else (zl > 0)

            @pl.when(there)
            def _():
                z_fwd(j, s, up).wait_recv()

                @pl.when(on)
                def _():
                    z_fwd(j, s, up).start()

    def st_y1(j):
        for k in range(1, ZL):
            s = (zl + k) % ZL
            y1(j, s, 1).start()
            y1(j, s, 0).start()

    def st_y2(j):
        y1_in(j, 1).wait_recv()
        y2(j, 1).start()
        y1_in(j, 0).wait_recv()
        y2(j, 0).start()

    def st_gemm(j):
        @pl.when(j == 0)
        def _():
            r_loc.wait()
            w_loc.wait()
            r_rem.wait_recv()

        y2_in(j).wait_recv()
        lhs = jnp.concatenate([lg[j, s] for s in range(TP)], axis=1)
        for n in range(4):
            rhs = rall[:, :, :, 256 * n : 256 * n + 256].reshape(TP * 2 * n_mem, 256)
            acc = jnp.dot(lhs, rhs, preferred_element_type=F32)
            part[j, :, :, :, 256 * n : 256 * n + 256] = acc.astype(BF16).reshape(X, ZH, DR, 256)
        rs1(j, 1).start()
        rs1(j, 0).start()

    def st_rs2(j):
        rs1(j, 1).wait_recv()
        part[j, xp, 0] = (part[j, xp, 0].astype(F32) + rh[j, 1].astype(F32)).astype(BF16)
        rs2(j, 1).start()
        rs1(j, 0).wait_recv()
        part[j, xm, 1] = (part[j, xm, 1].astype(F32) + rh[j, 0].astype(F32)).astype(BF16)
        rs2(j, 0).start()

    def st_sum(j):
        rs2_in(j).wait_recv()
        w = wv[j].astype(F32)
        for h in range(ZH):
            mine = part[j, x, h].astype(F32) + jnp.where(zh == h, w, 0.0)
            part[j, x, h] = (mine + rf[j, 1, h].astype(F32) + rf[j, 0, h].astype(F32)).astype(BF16)
        z4(j).start()
        drain_left(j)

    def st_fin(j):
        z4(j).wait_recv()
        for h in range(ZH):
            out[x, h, c, j] = (part[j, x, h].astype(F32) + zr[j, h].astype(F32)).astype(BF16)
        ag1(j, 1).start()
        ag1(j, 0).start()
        core(j, 0).start()
        drain_sums(j)

    def st_ag2(j):
        ag1(j, 1).wait_recv()
        ag2(j, 1).start()
        core(j, 3).start()
        ag1(j, 0).wait_recv()
        ag2(j, 0).start()
        core(j, 1).start()

    def st_last(j):
        ag2_in(j).wait_recv()
        core(j, 2).start()

        @pl.when(j >= 2)
        def _():
            drain_out(j - 2)

    stages = (
        st_own_z,
        st_own_y,
        functools.partial(st_z, 1),
        functools.partial(st_z, 2),
        functools.partial(st_z, 3),
        st_y1,
        st_y2,
        st_gemm,
        st_rs2,
        st_sum,
        st_fin,
        st_ag2,
        st_last,
    )

    def step(i, carry):
        word, counts = carry[0], carry[1:]
        now = lax.rem(word, 16)
        for n, fn in enumerate(stages):

            @pl.when(now == n)
            def _():
                fn(counts[n])

        return (lax.div(word, 16),) + tuple(
            jnp.where(now == n, count + 1, count) for n, count in enumerate(counts)
        )

    def group(g, counts):
        word = jnp.int32(ORDER[0])
        for k, w in enumerate(ORDER):
            word = jnp.where(g == k, jnp.int32(w), word)
        return lax.fori_loop(0, STEPS, step, (word,) + counts)[1:]

    lax.fori_loop(0, len(ORDER), group, (jnp.int32(0),) * len(stages))
    m_rem.wait_send()
    ranks_rem.wait_send()
    r_rem.wait_send()
    drain_out(J - 2)
    drain_out(J - 1)


def per_device(left_factors, right_factors, ranks, weight):
    n_mem, width = left_factors.shape
    members, cols = right_factors.shape
    total = members * lax.axis_size("pop")
    J = CHUNKS
    DR = weight.shape[0] // J
    dma = pltpu.SemaphoreType.DMA
    anyspace = pl.BlockSpec(memory_space=pl.ANY)
    vmem = pl.BlockSpec(memory_space=pltpu.VMEM)
    out = pl.pallas_call(
        functools.partial(kernel, total),
        out_shape=pltpu.VMEM((X, ZH, CORES, J, DR, cols), BF16),
        in_specs=[anyspace] * 4,
        out_specs=vmem,
        scratch_shapes=[
            pltpu.VMEM((2, 1, n_mem), jnp.int32),
            pltpu.VMEM((2, n_mem, width // 2), BF16),
            pltpu.VMEM((J, TP, 8 * DR, 2 * n_mem), BF16),
            pltpu.VMEM((TP, 2, n_mem, cols), BF16),
            pltpu.VMEM((J, DR, cols), BF16),
            pltpu.VMEM((J, X, ZH, DR, cols), BF16),
            pltpu.VMEM((J, 2, DR, cols), BF16),
            pltpu.VMEM((J, 2, ZH, DR, cols), BF16),
            pltpu.VMEM((J, ZH, DR, cols), BF16),
            dma((10,)),
            dma((J,)),
            dma((J, ZL)),
            dma((J,)),
            dma((J, 2)),
            dma((J,)),
            dma((J,)),
            dma((J, 2)),
            dma((J,)),
            dma((J,)),
            dma((J,)),
            dma((J,)),
            dma((J, 2)),
            dma((J,)),
            dma((J,)),
            dma((J,)),
        ],
        compiler_params=pltpu.CompilerParams(
            collective_id=0, has_side_effects=True, vmem_limit_bytes=48 * 2**20
        ),
    )(
        left_factors,
        ranks.reshape(1, n_mem),
        right_factors.reshape(TP, n_mem, cols),
        weight.reshape(J, DR, cols),
    )
    return out.reshape(X * ZH * CORES * J * DR, cols)


def solution(mesh):
    return jax.shard_map(
        per_device,
        mesh=mesh,
        in_specs=(P(("pop", "tp"), None), P("pop", "tp"), P(("pop", "tp")), P("pop", "tp")),
        out_specs=P(None, "tp"),
        check_vma=False,
    )
```

```python
import functools
import math

import jax
import jax.numpy as jnp
from jax import lax
from jax.experimental import pallas as pl
from jax.experimental.pallas import tpu as pltpu
from jax.sharding import PartitionSpec as P

MESH = pl.DeviceIdType.MESH
X, ZH, CORES, Y, ZL = 4, 2, 2, 4, 4
TP = Y * ZL
CHUNKS = 16
STEPS = 7
ORDER = (
    0x0110110, 0x1111010, 0x5403210, 0x5410302, 0x2256432, 0x5126430, 0x2203720, 0x2054736,
    0x4226383, 0x9607538, 0x6897354, 0x4873254, 0x0A56320, 0xA564897, 0xB368794, 0x689B475,
    0x6875A32, 0x82754A9, 0x6CB9113, 0x68375A4, 0x7C54BA9, 0xCA56481, 0x9AC8179, 0x6BB8796,
    0x79B879B, 0xAA89CA8, 0xC9CAB9A, 0xAACCBAB, 0xBBBCCBB, 0xFFCCCCC,
)
DIRECT = 4
F32, BF16 = jnp.float32, jnp.bfloat16


def kernel(
    total,
    left_in,
    ranks_in,
    right,
    weight,
    out,
    ranks,
    members,
    lg,
    rall,
    wv,
    part,
    rh,
    rf,
    zr,
    pre_sem,
    z_s,
    z_r,
    y_s,
    y1_r,
    y2_r,
    rs_s,
    rs1_r,
    rs2_r,
    z4_s,
    z4_r,
    ag_s,
    ag1_r,
    ag2_r,
    core_s,
    core_r,
):
    p, t = lax.axis_index("pop"), lax.axis_index("tp")
    x, zh, c = p // 4, (p // 2) % 2, p % 2
    y, zl = t // ZL, t % ZL
    xp, xm, xo = (x + 1) % 4, (x + 3) % 4, (x + 2) % 4
    yp, ym = (y + 1) % 4, (y + 3) % 4
    J = lg.shape[0]
    DR = part.shape[3]

    def dev(x_=x, zh_=zh, c_=c, y_=y, zl_=zl):
        return (x_ * 4 + zh_ * 2 + c_, y_ * ZL + zl_)

    def rcopy(src, dst, ssem, rsem, d):
        return pltpu.make_async_remote_copy(
            src_ref=src, dst_ref=dst, send_sem=ssem, recv_sem=rsem, device_id=d, device_id_type=MESH
        )

    d_xp, d_xm, d_yp, d_ym = dev(x_=xp), dev(x_=xm), dev(y_=yp), dev(y_=ym)
    d_z4, d_c = dev(zh_=1 - zh), dev(c_=1 - c)
    d_zu, d_zd = dev(zl_=jnp.minimum(zl + 1, ZL - 1)), dev(zl_=jnp.maximum(zl - 1, 0))

    r_loc = pltpu.make_async_copy(right, rall.at[:, c], pre_sem.at[0])
    w_loc = pltpu.make_async_copy(weight, wv, pre_sem.at[1])
    ranks_loc = pltpu.make_async_copy(ranks_in, ranks.at[c], pre_sem.at[2])
    ranks_loc.start()

    def left_block(m, half):
        return left_in.at[:, pl.ds(pl.multiple_of(256 * (2 * m + half), 256), 256)]

    for m in range(8):
        pltpu.make_async_copy(left_block(m, c), members.at[c, :, pl.ds(256 * m, 256)], pre_sem.at[3]).start()
    r_loc.start()
    w_loc.start()

    bar = pltpu.get_barrier_semaphore()
    for d in (d_xp, d_xm, d_yp, d_ym, d_z4, d_c):
        pl.semaphore_signal(bar, 1, device_id=d, device_id_type=MESH)

    for k in range(1, ZL):
        pl.semaphore_signal(bar, 1, device_id=dev(zl_=(zl + k) % ZL), device_id_type=MESH)

    pl.semaphore_wait(bar, 6 + ZL - 1)

    ranks_rem = rcopy(ranks_in, ranks.at[c], pre_sem.at[6], pre_sem.at[7], d_c)
    ranks_rem.start()
    for m in range(8):
        rcopy(left_block(m, 1 - c), members.at[c, :, pl.ds(256 * m, 256)], pre_sem.at[8], pre_sem.at[9], d_c).start()
    r_rem = rcopy(right, rall.at[:, c], pre_sem.at[4], pre_sem.at[5], d_c)
    r_rem.start()

    n_mem = left_in.shape[0]
    m_rem = rcopy(members.at[c], members.at[c], pre_sem.at[8], pre_sem.at[9], d_c)
    ranks_loc.wait()
    ranks_rem.wait_recv()
    eye = lax.broadcasted_iota(jnp.int32, (n_mem, n_mem), 0) == lax.broadcasted_iota(jnp.int32, (n_mem, n_mem), 1)
    scores = []
    for k in range(CORES):
        row = (2.0 * ranks[k].astype(F32) + 1.0 - total) / total * math.sqrt(3.0 / total)
        row = jnp.where(eye, jnp.broadcast_to(row, (n_mem, n_mem)), 0.0)
        scores.append(jnp.sum(row, axis=1, keepdims=True))
    score = jnp.concatenate(scores, axis=0)
    pltpu.make_async_copy(members.at[c], members.at[c], pre_sem.at[3]).wait()
    m_rem.wait_recv()
    for m in range(8):
        both = members[:, :, 256 * m : 256 * m + 256].reshape(2 * n_mem, 256).astype(F32)
        cols = (score * both).astype(BF16).astype(F32).T.astype(BF16)
        for j in range(J):
            lg[j, t, m * DR : (m + 1) * DR, :] = cols[j * DR : (j + 1) * DR]

    def z_own(j, up):
        ref = lg.at[j, t]
        return rcopy(ref, ref, z_s.at[j], z_r.at[j, zl], d_zu if up else d_zd)

    def z_direct(j, q):
        ref = lg.at[j, t]
        return rcopy(ref, ref, z_s.at[j], z_r.at[j, zl], dev(zl_=q))

    def z_fwd(j, s, up):
        ref = lg.at[j, y * ZL + s]
        return rcopy(ref, ref, z_s.at[j], z_r.at[j, s], d_zu if up else d_zd)

    def y1(j, s, plus):
        ref = lg.at[j, y * ZL + s]
        return rcopy(ref, ref, y_s.at[j], y1_r.at[j, plus], d_yp if plus else d_ym)

    def y1_in(j, plus):
        ref = lg.at[j, pl.ds((ym if plus else yp) * ZL, ZL)]
        return rcopy(ref, ref, y_s.at[j], y1_r.at[j, plus], d_yp if plus else d_ym)

    def y2(j, plus):
        b = ym * ZL if plus else yp * ZL + ZL // 2
        ref = lg.at[j, pl.ds(b, ZL // 2)]
        return rcopy(ref, ref, y_s.at[j], y2_r.at[j], d_yp if plus else d_ym)

    def y2_in(j):
        ref = lg.at[j, pl.ds(((y + 2) % 4) * ZL, ZL)]
        return rcopy(ref, ref, y_s.at[j], y2_r.at[j], d_yp)

    def rs1(j, plus):
        if plus:
            return rcopy(part.at[j, xo, 0], rh.at[j, 1], rs_s.at[j], rs1_r.at[j, 1], d_xp)
        return rcopy(part.at[j, xo, 1], rh.at[j, 0], rs_s.at[j], rs1_r.at[j, 0], d_xm)

    def rs2(j, plus):
        if plus:
            return rcopy(part.at[j, xp], rf.at[j, 1], rs_s.at[j], rs2_r.at[j], d_xp)
        return rcopy(part.at[j, xm], rf.at[j, 0], rs_s.at[j], rs2_r.at[j], d_xm)

    def rs2_in(j):
        return rcopy(rf.at[j], rf.at[j], rs_s.at[j], rs2_r.at[j], d_xp)

    def z4(j):
        return rcopy(part.at[j, x], zr.at[j], z4_s.at[j], z4_r.at[j], d_z4)

    def ag1(j, plus):
        ref = out.at[x, :, c, j]
        return rcopy(ref, ref, ag_s.at[j], ag1_r.at[j, plus], d_xp if plus else d_xm)

    def ag2(j, plus):
        ref = out.at[xm, 0, c, j] if plus else out.at[xp, 1, c, j]
        return rcopy(ref, ref, ag_s.at[j], ag2_r.at[j], d_xp if plus else d_xm)

    def ag2_in(j):
        ref = out.at[xo, :, c, j]
        return rcopy(ref, ref, ag_s.at[j], ag2_r.at[j], d_xp)

    def core(j, k):
        ref = out.at[(x + k) % 4, :, c, j]
        return rcopy(ref, ref, core_s.at[j], core_r.at[j], d_c)

    def drain_left(j):
        sent = lg.at[j, pl.ds(0, 3 * ZL)]
        rcopy(sent, sent, y_s.at[j], y2_r.at[j], d_yp).wait_send()
        line = j >= DIRECT
        edge = jnp.logical_or(zl == 0, zl == ZL - 1)
        inner = jnp.logical_not(edge)
        for n, here in ((3, j < DIRECT), (1, jnp.logical_and(line, edge)), (5, jnp.logical_and(line, inner))):

            @pl.when(here)
            def _():
                some = lg.at[j, pl.ds(0, n)]
                rcopy(some, some, z_s.at[j], z_r.at[j, 0], d_c).wait_send()

    def drain_sums(j):
        sent = part.at[j, pl.ds(0, 3)]
        rcopy(sent, sent, rs_s.at[j], rs2_r.at[j], d_xp).wait_send()

    def drain_out(j):
        sent = out.at[pl.ds(0, 3), :, c, j]
        rcopy(sent, sent, ag_s.at[j], ag2_r.at[j], d_xp).wait_send()
        z4(j).wait_send()
        sent = out.at[:, :, c, j]
        rcopy(sent, sent, core_s.at[j], core_r.at[j], d_c).wait_send()
        came = out.at[:, :, 1 - c, j]
        rcopy(came, came, core_s.at[j], core_r.at[j], d_c).wait_recv()

    def st_own_z(j):
        @pl.when(j < DIRECT)
        def _():
            for q in range(ZL):
                pl.when(zl != q)(lambda: z_direct(j, q).start())

        @pl.when(j >= DIRECT)
        def _():
            pl.when(zl < ZL - 1)(lambda: z_own(j, 1).start())
            pl.when(zl > 0)(lambda: z_own(j, 0).start())

    def st_own_y(j):
        y1(j, zl, 1).start()
        y1(j, zl, 0).start()

    def st_z(k, j):
        for up in (1, 0):
            s = zl - k if up else zl + k
            there = (s >= 0) if up else (s < ZL)
            on = jnp.logical_and(j >= DIRECT, (zl < ZL - 1) if up else (zl > 0))

            @pl.when(there)
            def _():
                z_fwd(j, s, up).wait_recv()

                @pl.when(on)
                def _():
                    z_fwd(j, s, up).start()

    def st_y1(j):
        for k in range(1, ZL):
            s = (zl + k) % ZL
            y1(j, s, 1).start()
            y1(j, s, 0).start()

    def st_y2(j):
        y1_in(j, 1).wait_recv()
        y2(j, 1).start()
        y1_in(j, 0).wait_recv()
        y2(j, 0).start()

    def st_gemm(j):
        @pl.when(j == 0)
        def _():
            r_loc.wait()
            w_loc.wait()
            r_rem.wait_recv()

        y2_in(j).wait_recv()
        lhs = jnp.concatenate([lg[j, s] for s in range(TP)], axis=1)
        for n in range(4):
            rhs = rall[:, :, :, 256 * n : 256 * n + 256].reshape(TP * 2 * n_mem, 256)
            acc = jnp.dot(lhs, rhs, preferred_element_type=F32)
            part[j, :, :, :, 256 * n : 256 * n + 256] = acc.astype(BF16).reshape(X, ZH, DR, 256)
        rs1(j, 1).start()
        rs1(j, 0).start()

    def st_rs2(j):
        rs1(j, 1).wait_recv()
        part[j, xp, 0] = (part[j, xp, 0].astype(F32) + rh[j, 1].astype(F32)).astype(BF16)
        rs2(j, 1).start()
        rs1(j, 0).wait_recv()
        part[j, xm, 1] = (part[j, xm, 1].astype(F32) + rh[j, 0].astype(F32)).astype(BF16)
        rs2(j, 0).start()

    def st_sum(j):
        rs2_in(j).wait_recv()
        w = wv[j].astype(F32)
        for h in range(ZH):
            mine = part[j, x, h].astype(F32) + jnp.where(zh == h, w, 0.0)
            part[j, x, h] = (mine + rf[j, 1, h].astype(F32) + rf[j, 0, h].astype(F32)).astype(BF16)
        z4(j).start()
        drain_left(j)

    def st_fin(j):
        z4(j).wait_recv()
        for h in range(ZH):
            out[x, h, c, j] = (part[j, x, h].astype(F32) + zr[j, h].astype(F32)).astype(BF16)
        ag1(j, 1).start()
        ag1(j, 0).start()
        core(j, 0).start()
        drain_sums(j)

    def st_ag2(j):
        ag1(j, 1).wait_recv()
        ag2(j, 1).start()
        core(j, 3).start()
        ag1(j, 0).wait_recv()
        ag2(j, 0).start()
        core(j, 1).start()

    def st_last(j):
        ag2_in(j).wait_recv()
        core(j, 2).start()

        @pl.when(j >= 2)
        def _():
            drain_out(j - 2)

    stages = (
        st_own_z,
        st_own_y,
        functools.partial(st_z, 1),
        functools.partial(st_z, 2),
        functools.partial(st_z, 3),
        st_y1,
        st_y2,
        st_gemm,
        st_rs2,
        st_sum,
        st_fin,
        st_ag2,
        st_last,
    )

    def step(i, carry):
        word, counts = carry[0], carry[1:]
        now = lax.rem(word, 16)
        for n, fn in enumerate(stages):

            @pl.when(now == n)
            def _():
                fn(counts[n])

        return (lax.div(word, 16),) + tuple(
            jnp.where(now == n, count + 1, count) for n, count in enumerate(counts)
        )

    def group(g, counts):
        word = jnp.int32(ORDER[0])
        for k, w in enumerate(ORDER):
            word = jnp.where(g == k, jnp.int32(w), word)
        return lax.fori_loop(0, STEPS, step, (word,) + counts)[1:]

    lax.fori_loop(0, len(ORDER), group, (jnp.int32(0),) * len(stages))
    m_rem.wait_send()
    ranks_rem.wait_send()
    r_rem.wait_send()
    drain_out(J - 2)
    drain_out(J - 1)


def per_device(left_factors, right_factors, ranks, weight):
    n_mem, width = left_factors.shape
    members, cols = right_factors.shape
    total = members * lax.axis_size("pop")
    J = CHUNKS
    DR = weight.shape[0] // J
    dma = pltpu.SemaphoreType.DMA
    anyspace = pl.BlockSpec(memory_space=pl.ANY)
    vmem = pl.BlockSpec(memory_space=pltpu.VMEM)
    out = pl.pallas_call(
        functools.partial(kernel, total),
        out_shape=pltpu.VMEM((X, ZH, CORES, J, DR, cols), BF16),
        in_specs=[anyspace] * 4,
        out_specs=vmem,
        scratch_shapes=[
            pltpu.VMEM((2, 1, n_mem), jnp.int32),
            pltpu.VMEM((2, n_mem, width // 2), BF16),
            pltpu.VMEM((J, TP, 8 * DR, 2 * n_mem), BF16),
            pltpu.VMEM((TP, 2, n_mem, cols), BF16),
            pltpu.VMEM((J, DR, cols), BF16),
            pltpu.VMEM((J, X, ZH, DR, cols), BF16),
            pltpu.VMEM((J, 2, DR, cols), BF16),
            pltpu.VMEM((J, 2, ZH, DR, cols), BF16),
            pltpu.VMEM((J, ZH, DR, cols), BF16),
            dma((10,)),
            dma((J,)),
            dma((J, ZL)),
            dma((J,)),
            dma((J, 2)),
            dma((J,)),
            dma((J,)),
            dma((J, 2)),
            dma((J,)),
            dma((J,)),
            dma((J,)),
            dma((J,)),
            dma((J, 2)),
            dma((J,)),
            dma((J,)),
            dma((J,)),
        ],
        compiler_params=pltpu.CompilerParams(
            collective_id=0, has_side_effects=True, vmem_limit_bytes=48 * 2**20
        ),
    )(
        left_factors,
        ranks.reshape(1, n_mem),
        right_factors.reshape(TP, n_mem, cols),
        weight.reshape(J, DR, cols),
    )
    return out.reshape(X * ZH * CORES * J * DR, cols)


def solution(mesh):
    return jax.shard_map(
        per_device,
        mesh=mesh,
        in_specs=(P(("pop", "tp"), None), P("pop", "tp"), P(("pop", "tp")), P("pop", "tp")),
        out_specs=P(None, "tp"),
        check_vma=False,
    )
```

```python
import functools
import math

import jax
import jax.numpy as jnp
from jax import lax
from jax.experimental import pallas as pl
from jax.experimental.pallas import tpu as pltpu
from jax.sharding import PartitionSpec as P

MESH = pl.DeviceIdType.MESH
X, ZH, CORES, Y, ZL = 4, 2, 2, 4, 4
TP = Y * ZL
CHUNKS = 16
STEPS = 7
ORDER = (
    0x0111110, 0x3210011, 0x3201054, 0x0600541, 0x6325432, 0x7520042, 0x0023162, 0x2654387,
    0x5437203, 0x8562498, 0x2436973, 0x469A875, 0xA234875, 0x87B3956, 0xA1B5469, 0x5426087,
    0x608793A, 0x51C4BA3, 0x1867B92, 0x8352A74, 0xA171B69, 0x6854B93, 0xBC58497, 0x6879A6C,
    0x79B879A, 0xBA989A8, 0xACACB9A, 0xCCBACAB, 0xCBBBCCB, 0xFFCCCCC,
)
DIRECT = 4
F32, BF16 = jnp.float32, jnp.bfloat16


def kernel(
    total,
    left_in,
    ranks_in,
    right,
    weight,
    out,
    ranks,
    members,
    lg,
    rall,
    wv,
    part,
    rh,
    rf,
    zr,
    pre_sem,
    z_s,
    z_r,
    y_s,
    y1_r,
    y2_r,
    rs_s,
    rs1_r,
    rs2_r,
    z4_s,
    z4_r,
    ag_s,
    ag1_r,
    ag2_r,
    core_s,
    core_r,
):
    p, t = lax.axis_index("pop"), lax.axis_index("tp")
    x, zh, c = p // 4, (p // 2) % 2, p % 2
    y, zl = t // ZL, t % ZL
    xp, xm, xo = (x + 1) % 4, (x + 3) % 4, (x + 2) % 4
    yp, ym = (y + 1) % 4, (y + 3) % 4
    J = lg.shape[0]
    DR = part.shape[3]

    def dev(x_=x, zh_=zh, c_=c, y_=y, zl_=zl):
        return (x_ * 4 + zh_ * 2 + c_, y_ * ZL + zl_)

    def rcopy(src, dst, ssem, rsem, d):
        return pltpu.make_async_remote_copy(
            src_ref=src, dst_ref=dst, send_sem=ssem, recv_sem=rsem, device_id=d, device_id_type=MESH
        )

    d_xp, d_xm, d_yp, d_ym = dev(x_=xp), dev(x_=xm), dev(y_=yp), dev(y_=ym)
    d_z4, d_c = dev(zh_=1 - zh), dev(c_=1 - c)
    d_zu, d_zd = dev(zl_=jnp.minimum(zl + 1, ZL - 1)), dev(zl_=jnp.maximum(zl - 1, 0))

    r_loc = pltpu.make_async_copy(right, rall.at[:, c], pre_sem.at[0])
    w_loc = pltpu.make_async_copy(weight, wv, pre_sem.at[1])
    ranks_loc = pltpu.make_async_copy(ranks_in, ranks.at[c], pre_sem.at[2])
    ranks_loc.start()

    def left_block(m, half):
        return left_in.at[:, pl.ds(pl.multiple_of(256 * (2 * m + half), 256), 256)]

    for m in range(8):
        pltpu.make_async_copy(left_block(m, c), members.at[c, :, pl.ds(256 * m, 256)], pre_sem.at[3]).start()
    r_loc.start()
    w_loc.start()

    bar = pltpu.get_barrier_semaphore()
    for d in (d_xp, d_xm, d_yp, d_ym, d_z4, d_c):
        pl.semaphore_signal(bar, 1, device_id=d, device_id_type=MESH)

    for k in range(1, ZL):
        pl.semaphore_signal(bar, 1, device_id=dev(zl_=(zl + k) % ZL), device_id_type=MESH)

    pl.semaphore_wait(bar, 6 + ZL - 1)

    ranks_rem = rcopy(ranks_in, ranks.at[c], pre_sem.at[6], pre_sem.at[7], d_c)
    ranks_rem.start()
    for m in range(8):
        rcopy(left_block(m, 1 - c), members.at[c, :, pl.ds(256 * m, 256)], pre_sem.at[8], pre_sem.at[9], d_c).start()
    r_rem = rcopy(right, rall.at[:, c], pre_sem.at[4], pre_sem.at[5], d_c)
    r_rem.start()

    n_mem = left_in.shape[0]
    m_rem = rcopy(members.at[c], members.at[c], pre_sem.at[8], pre_sem.at[9], d_c)
    ranks_loc.wait()
    ranks_rem.wait_recv()
    eye = lax.broadcasted_iota(jnp.int32, (n_mem, n_mem), 0) == lax.broadcasted_iota(jnp.int32, (n_mem, n_mem), 1)
    scores = []
    for k in range(CORES):
        row = (2.0 * ranks[k].astype(F32) + 1.0 - total) / total * math.sqrt(3.0 / total)
        row = jnp.where(eye, jnp.broadcast_to(row, (n_mem, n_mem)), 0.0)
        scores.append(jnp.sum(row, axis=1, keepdims=True))
    score = jnp.concatenate(scores, axis=0)
    pltpu.make_async_copy(members.at[c], members.at[c], pre_sem.at[3]).wait()
    m_rem.wait_recv()
    for m in range(8):
        both = members[:, :, 256 * m : 256 * m + 256].reshape(2 * n_mem, 256).astype(F32)
        cols = (score * both).astype(BF16).astype(F32).T.astype(BF16)
        for j in range(J):
            lg[j, t, m * DR : (m + 1) * DR, :] = cols[j * DR : (j + 1) * DR]

    def z_own(j, up):
        ref = lg.at[j, t]
        return rcopy(ref, ref, z_s.at[j], z_r.at[j, zl], d_zu if up else d_zd)

    def z_direct(j, q):
        ref = lg.at[j, t]
        return rcopy(ref, ref, z_s.at[j], z_r.at[j, zl], dev(zl_=q))

    def z_fwd(j, s, up):
        ref = lg.at[j, y * ZL + s]
        return rcopy(ref, ref, z_s.at[j], z_r.at[j, s], d_zu if up else d_zd)

    def y1(j, s, plus):
        ref = lg.at[j, y * ZL + s]
        return rcopy(ref, ref, y_s.at[j], y1_r.at[j, plus], d_yp if plus else d_ym)

    def y1_in(j, plus):
        ref = lg.at[j, pl.ds((ym if plus else yp) * ZL, ZL)]
        return rcopy(ref, ref, y_s.at[j], y1_r.at[j, plus], d_yp if plus else d_ym)

    def y2(j, plus):
        b = ym * ZL if plus else yp * ZL + ZL // 2
        ref = lg.at[j, pl.ds(b, ZL // 2)]
        return rcopy(ref, ref, y_s.at[j], y2_r.at[j], d_yp if plus else d_ym)

    def y2_in(j):
        ref = lg.at[j, pl.ds(((y + 2) % 4) * ZL, ZL)]
        return rcopy(ref, ref, y_s.at[j], y2_r.at[j], d_yp)

    def rs1(j, plus):
        if plus:
            return rcopy(part.at[j, xo, 0], rh.at[j, 1], rs_s.at[j], rs1_r.at[j, 1], d_xp)
        return rcopy(part.at[j, xo, 1], rh.at[j, 0], rs_s.at[j], rs1_r.at[j, 0], d_xm)

    def rs2(j, plus):
        if plus:
            return rcopy(part.at[j, xp], rf.at[j, 1], rs_s.at[j], rs2_r.at[j], d_xp)
        return rcopy(part.at[j, xm], rf.at[j, 0], rs_s.at[j], rs2_r.at[j], d_xm)

    def rs2_in(j):
        return rcopy(rf.at[j], rf.at[j], rs_s.at[j], rs2_r.at[j], d_xp)

    def z4(j):
        return rcopy(part.at[j, x], zr.at[j], z4_s.at[j], z4_r.at[j], d_z4)

    def ag1(j, plus):
        ref = out.at[x, :, c, j]
        return rcopy(ref, ref, ag_s.at[j], ag1_r.at[j, plus], d_xp if plus else d_xm)

    def ag2(j, plus):
        ref = out.at[xm, 0, c, j] if plus else out.at[xp, 1, c, j]
        return rcopy(ref, ref, ag_s.at[j], ag2_r.at[j], d_xp if plus else d_xm)

    def ag2_in(j):
        ref = out.at[xo, :, c, j]
        return rcopy(ref, ref, ag_s.at[j], ag2_r.at[j], d_xp)

    def core(j, k):
        ref = out.at[(x + k) % 4, :, c, j]
        return rcopy(ref, ref, core_s.at[j], core_r.at[j], d_c)

    def core_all(j):
        ref = out.at[:, :, c, j]
        return rcopy(ref, ref, core_s.at[j], core_r.at[j], d_c)

    def drain_left(j):
        sent = lg.at[j, pl.ds(0, 3 * ZL)]
        rcopy(sent, sent, y_s.at[j], y2_r.at[j], d_yp).wait_send()
        line = j >= DIRECT
        edge = jnp.logical_or(zl == 0, zl == ZL - 1)
        inner = jnp.logical_not(edge)
        for n, here in ((3, j < DIRECT), (1, jnp.logical_and(line, edge)), (5, jnp.logical_and(line, inner))):

            @pl.when(here)
            def _():
                some = lg.at[j, pl.ds(0, n)]
                rcopy(some, some, z_s.at[j], z_r.at[j, 0], d_c).wait_send()

    def drain_sums(j):
        sent = part.at[j, pl.ds(0, 3)]
        rcopy(sent, sent, rs_s.at[j], rs2_r.at[j], d_xp).wait_send()

    def drain_out(j):
        sent = out.at[pl.ds(0, 3), :, c, j]
        rcopy(sent, sent, ag_s.at[j], ag2_r.at[j], d_xp).wait_send()
        z4(j).wait_send()
        sent = out.at[:, :, c, j]
        rcopy(sent, sent, core_s.at[j], core_r.at[j], d_c).wait_send()
        came = out.at[:, :, 1 - c, j]
        rcopy(came, came, core_s.at[j], core_r.at[j], d_c).wait_recv()

    def st_own_z(j):
        @pl.when(j < DIRECT)
        def _():
            for q in range(ZL):
                pl.when(zl != q)(lambda: z_direct(j, q).start())

        @pl.when(j >= DIRECT)
        def _():
            pl.when(zl < ZL - 1)(lambda: z_own(j, 1).start())
            pl.when(zl > 0)(lambda: z_own(j, 0).start())

    def st_own_y(j):
        y1(j, zl, 1).start()
        y1(j, zl, 0).start()

    def st_z(k, j):
        for up in (1, 0):
            s = zl - k if up else zl + k
            there = (s >= 0) if up else (s < ZL)
            on = jnp.logical_and(j >= DIRECT, (zl < ZL - 1) if up else (zl > 0))

            @pl.when(there)
            def _():
                z_fwd(j, s, up).wait_recv()

                @pl.when(on)
                def _():
                    z_fwd(j, s, up).start()

    def st_y1(j):
        for k in range(1, ZL):
            s = (zl + k) % ZL
            y1(j, s, 1).start()
            y1(j, s, 0).start()

    def st_y2(j):
        y1_in(j, 1).wait_recv()
        y2(j, 1).start()
        y1_in(j, 0).wait_recv()
        y2(j, 0).start()

    def st_gemm(j):
        @pl.when(j == 0)
        def _():
            r_loc.wait()
            w_loc.wait()
            r_rem.wait_recv()

        y2_in(j).wait_recv()
        lhs = jnp.concatenate([lg[j, s] for s in range(TP)], axis=1)
        for n in range(4):
            rhs = rall[:, :, :, 256 * n : 256 * n + 256].reshape(TP * 2 * n_mem, 256)
            acc = jnp.dot(lhs, rhs, preferred_element_type=F32)
            part[j, :, :, :, 256 * n : 256 * n + 256] = acc.astype(BF16).reshape(X, ZH, DR, 256)
        rs1(j, 1).start()
        rs1(j, 0).start()

    def st_rs2(j):
        rs1(j, 1).wait_recv()
        part[j, xp, 0] = (part[j, xp, 0].astype(F32) + rh[j, 1].astype(F32)).astype(BF16)
        rs2(j, 1).start()
        rs1(j, 0).wait_recv()
        part[j, xm, 1] = (part[j, xm, 1].astype(F32) + rh[j, 0].astype(F32)).astype(BF16)
        rs2(j, 0).start()

    def st_sum(j):
        rs2_in(j).wait_recv()
        w = wv[j].astype(F32)
        for h in range(ZH):
            mine = part[j, x, h].astype(F32) + jnp.where(zh == h, w, 0.0)
            part[j, x, h] = (mine + rf[j, 1, h].astype(F32) + rf[j, 0, h].astype(F32)).astype(BF16)
        z4(j).start()
        drain_left(j)

    def st_fin(j):
        z4(j).wait_recv()
        for h in range(ZH):
            out[x, h, c, j] = (part[j, x, h].astype(F32) + zr[j, h].astype(F32)).astype(BF16)
        ag1(j, 1).start()
        ag1(j, 0).start()
        pl.when(j >= J - 2)(lambda: core(j, 0).start())
        drain_sums(j)

    def st_ag2(j):
        ag1(j, 1).wait_recv()
        ag2(j, 1).start()
        ag1(j, 0).wait_recv()
        ag2(j, 0).start()

        @pl.when(j >= J - 2)
        def _():
            core(j, 3).start()
            core(j, 1).start()

    def st_last(j):
        ag2_in(j).wait_recv()
        pl.when(j >= J - 2)(lambda: core(j, 2).start())
        pl.when(j < J - 2)(lambda: core_all(j).start())
        pl.when(j >= 2)(lambda: drain_out(j - 2))

    stages = (
        st_own_z,
        st_own_y,
        functools.partial(st_z, 1),
        functools.partial(st_z, 2),
        functools.partial(st_z, 3),
        st_y1,
        st_y2,
        st_gemm,
        st_rs2,
        st_sum,
        st_fin,
        st_ag2,
        st_last,
    )

    def step(i, carry):
        word, counts = carry[0], carry[1:]
        now = lax.rem(word, 16)
        for n, fn in enumerate(stages):

            @pl.when(now == n)
            def _():
                fn(counts[n])

        return (lax.div(word, 16),) + tuple(
            jnp.where(now == n, count + 1, count) for n, count in enumerate(counts)
        )

    def group(g, counts):
        word = jnp.int32(ORDER[0])
        for k, w in enumerate(ORDER):
            word = jnp.where(g == k, jnp.int32(w), word)
        return lax.fori_loop(0, STEPS, step, (word,) + counts)[1:]

    lax.fori_loop(0, len(ORDER), group, (jnp.int32(0),) * len(stages))
    m_rem.wait_send()
    ranks_rem.wait_send()
    r_rem.wait_send()
    drain_out(J - 2)
    drain_out(J - 1)


def per_device(left_factors, right_factors, ranks, weight):
    n_mem, width = left_factors.shape
    members, cols = right_factors.shape
    total = members * lax.axis_size("pop")
    J = CHUNKS
    DR = weight.shape[0] // J
    dma = pltpu.SemaphoreType.DMA
    anyspace = pl.BlockSpec(memory_space=pl.ANY)
    vmem = pl.BlockSpec(memory_space=pltpu.VMEM)
    out = pl.pallas_call(
        functools.partial(kernel, total),
        out_shape=pltpu.VMEM((X, ZH, CORES, J, DR, cols), BF16),
        in_specs=[anyspace] * 4,
        out_specs=vmem,
        scratch_shapes=[
            pltpu.VMEM((2, 1, n_mem), jnp.int32),
            pltpu.VMEM((2, n_mem, width // 2), BF16),
            pltpu.VMEM((J, TP, 8 * DR, 2 * n_mem), BF16),
            pltpu.VMEM((TP, 2, n_mem, cols), BF16),
            pltpu.VMEM((J, DR, cols), BF16),
            pltpu.VMEM((J, X, ZH, DR, cols), BF16),
            pltpu.VMEM((J, 2, DR, cols), BF16),
            pltpu.VMEM((J, 2, ZH, DR, cols), BF16),
            pltpu.VMEM((J, ZH, DR, cols), BF16),
            dma((10,)),
            dma((J,)),
            dma((J, ZL)),
            dma((J,)),
            dma((J, 2)),
            dma((J,)),
            dma((J,)),
            dma((J, 2)),
            dma((J,)),
            dma((J,)),
            dma((J,)),
            dma((J,)),
            dma((J, 2)),
            dma((J,)),
            dma((J,)),
            dma((J,)),
        ],
        compiler_params=pltpu.CompilerParams(
            collective_id=0, has_side_effects=True, vmem_limit_bytes=48 * 2**20
        ),
    )(
        left_factors,
        ranks.reshape(1, n_mem),
        right_factors.reshape(TP, n_mem, cols),
        weight.reshape(J, DR, cols),
    )
    return out.reshape(X * ZH * CORES * J * DR, cols)


def solution(mesh):
    return jax.shard_map(
        per_device,
        mesh=mesh,
        in_specs=(P(("pop", "tp"), None), P("pop", "tp"), P(("pop", "tp")), P("pop", "tp")),
        out_specs=P(None, "tp"),
        check_vma=False,
    )
```

```python
import functools
import math

import jax
import jax.numpy as jnp
from jax import lax
from jax.experimental import pallas as pl
from jax.experimental.pallas import tpu as pltpu
from jax.sharding import PartitionSpec as P

MESH = pl.DeviceIdType.MESH
X, ZH, CORES, Y, ZL = 4, 2, 2, 4, 4
TP = Y * ZL
CHUNKS = 16
STEPS = 7
ORDER = (
    0x1111101, 0x0101010, 0x0015432, 0x1252432, 0x2132060, 0x5402630, 0x5473203, 0x5406227,
    0x3823348, 0x6497506, 0x2834795, 0x8725036, 0x72596A4, 0x52968A4, 0xB87B433, 0x73A9605,
    0x3514986, 0xB78546A, 0x6AB9472, 0x8317485, 0x91B796A, 0x817A568, 0xC67B549, 0x79869A8,
    0x8C7C9BA, 0xCCB89AC, 0x9AAAB9C, 0xBAABBAC, 0xBBBCCCB, 0xFFCCCCC,
)
DIRECT = 2
F32, BF16 = jnp.float32, jnp.bfloat16


def kernel(
    total,
    left_in,
    ranks_in,
    right,
    weight,
    out,
    ranks,
    members,
    lg,
    rall,
    wv,
    part,
    rh,
    rf,
    zr,
    pre_sem,
    z_s,
    z_r,
    y_s,
    y1_r,
    y2_r,
    rs_s,
    rs1_r,
    rs2_r,
    z4_s,
    z4_r,
    ag_s,
    ag1_r,
    ag2_r,
    core_s,
    core_r,
):
    p, t = lax.axis_index("pop"), lax.axis_index("tp")
    x, zh, c = p // 4, (p // 2) % 2, p % 2
    y, zl = t // ZL, t % ZL
    xp, xm, xo = (x + 1) % 4, (x + 3) % 4, (x + 2) % 4
    yp, ym = (y + 1) % 4, (y + 3) % 4
    J = lg.shape[0]
    DR = part.shape[3]

    def dev(x_=x, zh_=zh, c_=c, y_=y, zl_=zl):
        return (x_ * 4 + zh_ * 2 + c_, y_ * ZL + zl_)

    def rcopy(src, dst, ssem, rsem, d):
        return pltpu.make_async_remote_copy(
            src_ref=src, dst_ref=dst, send_sem=ssem, recv_sem=rsem, device_id=d, device_id_type=MESH
        )

    d_xp, d_xm, d_yp, d_ym = dev(x_=xp), dev(x_=xm), dev(y_=yp), dev(y_=ym)
    d_z4, d_c = dev(zh_=1 - zh), dev(c_=1 - c)
    d_zu, d_zd = dev(zl_=jnp.minimum(zl + 1, ZL - 1)), dev(zl_=jnp.maximum(zl - 1, 0))

    bar = pltpu.get_barrier_semaphore()
    for d in (d_xp, d_xm, d_yp, d_ym, d_z4, d_c):
        pl.semaphore_signal(bar, 1, device_id=d, device_id_type=MESH)

    for k in range(1, ZL):
        pl.semaphore_signal(bar, 1, device_id=dev(zl_=(zl + k) % ZL), device_id_type=MESH)

    ranks_loc = pltpu.make_async_copy(ranks_in, ranks.at[c], pre_sem.at[2])
    ranks_loc.start()

    def left_block(m, half):
        return left_in.at[:, pl.ds(pl.multiple_of(256 * (2 * m + half), 256), 256)]

    for m in range(8):
        pltpu.make_async_copy(left_block(m, c), members.at[c, :, pl.ds(256 * m, 256)], pre_sem.at[3]).start()

    pl.semaphore_wait(bar, 6 + ZL - 1)

    ranks_rem = rcopy(ranks_in, ranks.at[c], pre_sem.at[6], pre_sem.at[7], d_c)
    ranks_rem.start()
    for m in range(8):
        rcopy(left_block(m, 1 - c), members.at[c, :, pl.ds(256 * m, 256)], pre_sem.at[8], pre_sem.at[9], d_c).start()
    r_rem = rcopy(right, rall.at[:, c], pre_sem.at[4], pre_sem.at[5], d_c)
    r_loc = pltpu.make_async_copy(right, rall.at[:, c], pre_sem.at[0])
    w_loc = pltpu.make_async_copy(weight, wv, pre_sem.at[1])
    r_rem.start()
    r_loc.start()
    w_loc.start()

    n_mem = left_in.shape[0]
    m_rem = rcopy(members.at[c], members.at[c], pre_sem.at[8], pre_sem.at[9], d_c)
    ranks_loc.wait()
    ranks_rem.wait_recv()
    eye = lax.broadcasted_iota(jnp.int32, (n_mem, n_mem), 0) == lax.broadcasted_iota(jnp.int32, (n_mem, n_mem), 1)
    scores = []
    for k in range(CORES):
        row = (2.0 * ranks[k].astype(F32) + 1.0 - total) / total * math.sqrt(3.0 / total)
        row = jnp.where(eye, jnp.broadcast_to(row, (n_mem, n_mem)), 0.0)
        scores.append(jnp.sum(row, axis=1, keepdims=True))
    score = jnp.concatenate(scores, axis=0)
    pltpu.make_async_copy(members.at[c], members.at[c], pre_sem.at[3]).wait()
    m_rem.wait_recv()
    for m in range(8):
        both = members[:, :, 256 * m : 256 * m + 256].reshape(2 * n_mem, 256).astype(F32)
        cols = (score * both).astype(BF16).astype(F32).T.astype(BF16)
        for j in range(J):
            lg[j, t, m * DR : (m + 1) * DR, :] = cols[j * DR : (j + 1) * DR]

    def z_own(j, up):
        ref = lg.at[j, t]
        return rcopy(ref, ref, z_s.at[j], z_r.at[j, zl], d_zu if up else d_zd)

    def z_direct(j, q):
        ref = lg.at[j, t]
        return rcopy(ref, ref, z_s.at[j], z_r.at[j, zl], dev(zl_=q))

    def z_fwd(j, s, up):
        ref = lg.at[j, y * ZL + s]
        return rcopy(ref, ref, z_s.at[j], z_r.at[j, s], d_zu if up else d_zd)

    def y1(j, s, plus):
        ref = lg.at[j, y * ZL + s]
        return rcopy(ref, ref, y_s.at[j], y1_r.at[j, plus], d_yp if plus else d_ym)

    def y1_in(j, plus):
        ref = lg.at[j, pl.ds((ym if plus else yp) * ZL, ZL)]
        return rcopy(ref, ref, y_s.at[j], y1_r.at[j, plus], d_yp if plus else d_ym)

    def y2(j, plus):
        b = ym * ZL if plus else yp * ZL + ZL // 2
        ref = lg.at[j, pl.ds(b, ZL // 2)]
        return rcopy(ref, ref, y_s.at[j], y2_r.at[j], d_yp if plus else d_ym)

    def y2_in(j):
        ref = lg.at[j, pl.ds(((y + 2) % 4) * ZL, ZL)]
        return rcopy(ref, ref, y_s.at[j], y2_r.at[j], d_yp)

    def rs1(j, plus):
        if plus:
            return rcopy(part.at[j, xo, 0], rh.at[j, 1], rs_s.at[j], rs1_r.at[j, 1], d_xp)
        return rcopy(part.at[j, xo, 1], rh.at[j, 0], rs_s.at[j], rs1_r.at[j, 0], d_xm)

    def rs2(j, plus):
        if plus:
            return rcopy(part.at[j, xp], rf.at[j, 1], rs_s.at[j], rs2_r.at[j], d_xp)
        return rcopy(part.at[j, xm], rf.at[j, 0], rs_s.at[j], rs2_r.at[j], d_xm)

    def rs2_in(j):
        return rcopy(rf.at[j], rf.at[j], rs_s.at[j], rs2_r.at[j], d_xp)

    def z4(j):
        return rcopy(part.at[j, x], zr.at[j], z4_s.at[j], z4_r.at[j], d_z4)

    def ag1(j, plus):
        ref = out.at[x, :, c, j]
        return rcopy(ref, ref, ag_s.at[j], ag1_r.at[j, plus], d_xp if plus else d_xm)

    def ag2(j, plus):
        ref = out.at[xm, 0, c, j] if plus else out.at[xp, 1, c, j]
        return rcopy(ref, ref, ag_s.at[j], ag2_r.at[j], d_xp if plus else d_xm)

    def ag2_in(j):
        ref = out.at[xo, :, c, j]
        return rcopy(ref, ref, ag_s.at[j], ag2_r.at[j], d_xp)

    def core(j, k):
        ref = out.at[(x + k) % 4, :, c, j]
        return rcopy(ref, ref, core_s.at[j], core_r.at[j], d_c)

    def core_all(j):
        ref = out.at[:, :, c, j]
        return rcopy(ref, ref, core_s.at[j], core_r.at[j], d_c)

    def drain_left(j):
        sent = lg.at[j, pl.ds(0, 3 * ZL)]
        rcopy(sent, sent, y_s.at[j], y2_r.at[j], d_yp).wait_send()
        line = j >= DIRECT
        edge = jnp.logical_or(zl == 0, zl == ZL - 1)
        inner = jnp.logical_not(edge)
        for n, here in ((3, j < DIRECT), (1, jnp.logical_and(line, edge)), (5, jnp.logical_and(line, inner))):

            @pl.when(here)
            def _():
                some = lg.at[j, pl.ds(0, n)]
                rcopy(some, some, z_s.at[j], z_r.at[j, 0], d_c).wait_send()

    def drain_sums(j):
        sent = part.at[j, pl.ds(0, 3)]
        rcopy(sent, sent, rs_s.at[j], rs2_r.at[j], d_xp).wait_send()

    def drain_out(j):
        sent = out.at[pl.ds(0, 3), :, c, j]
        rcopy(sent, sent, ag_s.at[j], ag2_r.at[j], d_xp).wait_send()
        z4(j).wait_send()
        sent = out.at[:, :, c, j]
        rcopy(sent, sent, core_s.at[j], core_r.at[j], d_c).wait_send()
        came = out.at[:, :, 1 - c, j]
        rcopy(came, came, core_s.at[j], core_r.at[j], d_c).wait_recv()

    def st_own_z(j):
        @pl.when(j < DIRECT)
        def _():
            for q in range(ZL):
                pl.when(zl != q)(lambda: z_direct(j, q).start())

        @pl.when(j >= DIRECT)
        def _():
            pl.when(zl < ZL - 1)(lambda: z_own(j, 1).start())
            pl.when(zl > 0)(lambda: z_own(j, 0).start())

    def st_own_y(j):
        y1(j, zl, 1).start()
        y1(j, zl, 0).start()

    def st_z(k, j):
        for up in (1, 0):
            s = zl - k if up else zl + k
            there = (s >= 0) if up else (s < ZL)
            on = jnp.logical_and(j >= DIRECT, (zl < ZL - 1) if up else (zl > 0))

            @pl.when(there)
            def _():
                z_fwd(j, s, up).wait_recv()

                @pl.when(on)
                def _():
                    z_fwd(j, s, up).start()

    def st_y1(j):
        for k in range(1, ZL):
            s = (zl + k) % ZL
            y1(j, s, 1).start()
            y1(j, s, 0).start()

    def st_y2(j):
        y1_in(j, 1).wait_recv()
        y2(j, 1).start()
        y1_in(j, 0).wait_recv()
        y2(j, 0).start()

    def st_gemm(j):
        @pl.when(j == 0)
        def _():
            r_loc.wait()
            w_loc.wait()
            r_rem.wait_recv()

        y2_in(j).wait_recv()
        lhs = jnp.concatenate([lg[j, s] for s in range(TP)], axis=1)
        for n in range(4):
            rhs = rall[:, :, :, 256 * n : 256 * n + 256].reshape(TP * 2 * n_mem, 256)
            acc = jnp.dot(lhs, rhs, preferred_element_type=F32)
            part[j, :, :, :, 256 * n : 256 * n + 256] = acc.astype(BF16).reshape(X, ZH, DR, 256)
        rs1(j, 1).start()
        rs1(j, 0).start()

    def st_rs2(j):
        rs1(j, 1).wait_recv()
        part[j, xp, 0] = (part[j, xp, 0].astype(F32) + rh[j, 1].astype(F32)).astype(BF16)
        rs2(j, 1).start()
        rs1(j, 0).wait_recv()
        part[j, xm, 1] = (part[j, xm, 1].astype(F32) + rh[j, 0].astype(F32)).astype(BF16)
        rs2(j, 0).start()

    def st_sum(j):
        rs2_in(j).wait_recv()
        w = wv[j].astype(F32)
        for h in range(ZH):
            mine = part[j, x, h].astype(F32) + jnp.where(zh == h, w, 0.0)
            part[j, x, h] = (mine + rf[j, 1, h].astype(F32) + rf[j, 0, h].astype(F32)).astype(BF16)
        z4(j).start()
        drain_left(j)

    def st_fin(j):
        z4(j).wait_recv()
        for h in range(ZH):
            out[x, h, c, j] = (part[j, x, h].astype(F32) + zr[j, h].astype(F32)).astype(BF16)
        ag1(j, 1).start()
        ag1(j, 0).start()
        pl.when(j >= J - 2)(lambda: core(j, 0).start())
        drain_sums(j)

    def st_ag2(j):
        ag1(j, 1).wait_recv()
        ag2(j, 1).start()
        ag1(j, 0).wait_recv()
        ag2(j, 0).start()

        @pl.when(j >= J - 2)
        def _():
            core(j, 3).start()
            core(j, 1).start()

    def st_last(j):
        ag2_in(j).wait_recv()
        pl.when(j >= J - 2)(lambda: core(j, 2).start())
        pl.when(j < J - 2)(lambda: core_all(j).start())
        pl.when(j >= 2)(lambda: drain_out(j - 2))

    stages = (
        st_own_z,
        st_own_y,
        functools.partial(st_z, 1),
        functools.partial(st_z, 2),
        functools.partial(st_z, 3),
        st_y1,
        st_y2,
        st_gemm,
        st_rs2,
        st_sum,
        st_fin,
        st_ag2,
        st_last,
    )

    def step(i, carry):
        word, counts = carry[0], carry[1:]
        now = lax.rem(word, 16)
        for n, fn in enumerate(stages):

            @pl.when(now == n)
            def _():
                fn(counts[n])

        return (lax.div(word, 16),) + tuple(
            jnp.where(now == n, count + 1, count) for n, count in enumerate(counts)
        )

    def group(g, counts):
        word = jnp.int32(ORDER[0])
        for k, w in enumerate(ORDER):
            word = jnp.where(g == k, jnp.int32(w), word)
        return lax.fori_loop(0, STEPS, step, (word,) + counts)[1:]

    lax.fori_loop(0, len(ORDER), group, (jnp.int32(0),) * len(stages))
    m_rem.wait_send()
    ranks_rem.wait_send()
    r_rem.wait_send()
    drain_out(J - 2)
    drain_out(J - 1)


def per_device(left_factors, right_factors, ranks, weight):
    n_mem, width = left_factors.shape
    members, cols = right_factors.shape
    total = members * lax.axis_size("pop")
    J = CHUNKS
    DR = weight.shape[0] // J
    dma = pltpu.SemaphoreType.DMA
    anyspace = pl.BlockSpec(memory_space=pl.ANY)
    vmem = pl.BlockSpec(memory_space=pltpu.VMEM)
    out = pl.pallas_call(
        functools.partial(kernel, total),
        out_shape=pltpu.VMEM((X, ZH, CORES, J, DR, cols), BF16),
        in_specs=[anyspace] * 4,
        out_specs=vmem,
        scratch_shapes=[
            pltpu.VMEM((2, 1, n_mem), jnp.int32),
            pltpu.VMEM((2, n_mem, width // 2), BF16),
            pltpu.VMEM((J, TP, 8 * DR, 2 * n_mem), BF16),
            pltpu.VMEM((TP, 2, n_mem, cols), BF16),
            pltpu.VMEM((J, DR, cols), BF16),
            pltpu.VMEM((J, X, ZH, DR, cols), BF16),
            pltpu.VMEM((J, 2, DR, cols), BF16),
            pltpu.VMEM((J, 2, ZH, DR, cols), BF16),
            pltpu.VMEM((J, ZH, DR, cols), BF16),
            dma((10,)),
            dma((J,)),
            dma((J, ZL)),
            dma((J,)),
            dma((J, 2)),
            dma((J,)),
            dma((J,)),
            dma((J, 2)),
            dma((J,)),
            dma((J,)),
            dma((J,)),
            dma((J,)),
            dma((J, 2)),
            dma((J,)),
            dma((J,)),
            dma((J,)),
        ],
        compiler_params=pltpu.CompilerParams(
            collective_id=0, has_side_effects=True, vmem_limit_bytes=48 * 2**20
        ),
    )(
        left_factors,
        ranks.reshape(1, n_mem),
        right_factors.reshape(TP, n_mem, cols),
        weight.reshape(J, DR, cols),
    )
    return out.reshape(X * ZH * CORES * J * DR, cols)


def solution(mesh):
    return jax.shard_map(
        per_device,
        mesh=mesh,
        in_specs=(P(("pop", "tp"), None), P("pop", "tp"), P(("pop", "tp")), P("pop", "tp")),
        out_specs=P(None, "tp"),
        check_vma=False,
    )
```

```python
import functools
import math

import jax
import jax.numpy as jnp
from jax import lax
from jax.experimental import pallas as pl
from jax.experimental.pallas import tpu as pltpu
from jax.sharding import PartitionSpec as P

MESH = pl.DeviceIdType.MESH
X, ZH, CORES, Y, ZL = 4, 2, 2, 4, 4
TP = Y * ZL
CHUNKS = 16
STEPS = 7
ORDER = (
    0x1111101, 0x0101010, 0x0015432, 0x1252432, 0x2132060, 0x5402630, 0x5473203, 0x5406227,
    0x3823348, 0x6497506, 0x2834795, 0x8725036, 0x72596A4, 0x52968A4, 0xB87B433, 0x73A9605,
    0x3514986, 0xB78546A, 0x6AB9472, 0x8317485, 0x91B796A, 0x817A568, 0xC67B549, 0x79869A8,
    0x8C7C9BA, 0xCCB89AC, 0x9AAAB9C, 0xBAABBAC, 0xBBBCCCB, 0xFFCCCCC,
)
DIRECT = 2
F32, BF16 = jnp.float32, jnp.bfloat16


def kernel(
    total,
    left_in,
    ranks_in,
    right,
    weight,
    out,
    ranks,
    members,
    lg,
    rall,
    wv,
    part,
    rh,
    rf,
    zr,
    pre_sem,
    z_s,
    z_r,
    y_s,
    y1_r,
    y2_r,
    rs_s,
    rs1_r,
    rs2_r,
    z4_s,
    z4_r,
    ag_s,
    ag1_r,
    ag2_r,
    core_s,
    core_r,
):
    p, t = lax.axis_index("pop"), lax.axis_index("tp")
    x, zh, c = p // 4, (p // 2) % 2, p % 2
    y, zl = t // ZL, t % ZL
    xp, xm, xo = (x + 1) % 4, (x + 3) % 4, (x + 2) % 4
    yp, ym = (y + 1) % 4, (y + 3) % 4
    J = lg.shape[0]
    DR = part.shape[3]

    def dev(x_=x, zh_=zh, c_=c, y_=y, zl_=zl):
        return (x_ * 4 + zh_ * 2 + c_, y_ * ZL + zl_)

    def rcopy(src, dst, ssem, rsem, d):
        return pltpu.make_async_remote_copy(
            src_ref=src, dst_ref=dst, send_sem=ssem, recv_sem=rsem, device_id=d, device_id_type=MESH
        )

    d_xp, d_xm, d_yp, d_ym = dev(x_=xp), dev(x_=xm), dev(y_=yp), dev(y_=ym)
    d_z4, d_c = dev(zh_=1 - zh), dev(c_=1 - c)
    d_zu, d_zd = dev(zl_=jnp.minimum(zl + 1, ZL - 1)), dev(zl_=jnp.maximum(zl - 1, 0))

    bar = pltpu.get_barrier_semaphore()
    for d in (d_xp, d_xm, d_yp, d_ym, d_z4, d_c):
        pl.semaphore_signal(bar, 1, device_id=d, device_id_type=MESH)

    for k in range(1, ZL):
        pl.semaphore_signal(bar, 1, device_id=dev(zl_=(zl + k) % ZL), device_id_type=MESH)

    ranks_loc = pltpu.make_async_copy(ranks_in, ranks.at[c], pre_sem.at[2])
    ranks_loc.start()

    def left_block(m, half):
        return left_in.at[:, pl.ds(pl.multiple_of(256 * (2 * m + half), 256), 256)]

    for m in range(8):
        pltpu.make_async_copy(left_block(m, c), members.at[c, :, pl.ds(256 * m, 256)], pre_sem.at[3]).start()

    pl.semaphore_wait(bar, 6 + ZL - 1)

    ranks_rem = rcopy(ranks_in, ranks.at[c], pre_sem.at[6], pre_sem.at[7], d_c)
    ranks_rem.start()
    for m in range(8):
        rcopy(left_block(m, 1 - c), members.at[c, :, pl.ds(256 * m, 256)], pre_sem.at[8], pre_sem.at[9], d_c).start()
    r_rem = rcopy(right, rall.at[:, c], pre_sem.at[4], pre_sem.at[5], d_c)
    r_loc = pltpu.make_async_copy(right, rall.at[:, c], pre_sem.at[0])
    w_loc = pltpu.make_async_copy(weight, wv, pre_sem.at[1])
    r_rem.start()
    r_loc.start()
    w_loc.start()

    n_mem = left_in.shape[0]
    m_rem = rcopy(members.at[c], members.at[c], pre_sem.at[8], pre_sem.at[9], d_c)
    ranks_loc.wait()
    ranks_rem.wait_recv()
    eye = lax.broadcasted_iota(jnp.int32, (n_mem, n_mem), 0) == lax.broadcasted_iota(jnp.int32, (n_mem, n_mem), 1)
    scores = []
    for k in range(CORES):
        row = (2.0 * ranks[k].astype(F32) + 1.0 - total) / total * math.sqrt(3.0 / total)
        row = jnp.where(eye, jnp.broadcast_to(row, (n_mem, n_mem)), 0.0)
        scores.append(jnp.sum(row, axis=1, keepdims=True))
    score = jnp.concatenate(scores, axis=0)
    pltpu.make_async_copy(members.at[c], members.at[c], pre_sem.at[3]).wait()
    m_rem.wait_recv()
    for m in range(8):
        both = members[:, :, 256 * m : 256 * m + 256].reshape(2 * n_mem, 256).astype(F32)
        cols = (score * both).astype(BF16).astype(F32).T.astype(BF16)
        for j in range(J):
            lg[j, t, m * DR : (m + 1) * DR, :] = cols[j * DR : (j + 1) * DR]

    def z_own(j, up):
        ref = lg.at[j, t]
        return rcopy(ref, ref, z_s.at[j], z_r.at[j, zl], d_zu if up else d_zd)

    def z_direct(j, q):
        ref = lg.at[j, t]
        return rcopy(ref, ref, z_s.at[j], z_r.at[j, zl], dev(zl_=q))

    def z_fwd(j, s, up):
        ref = lg.at[j, y * ZL + s]
        return rcopy(ref, ref, z_s.at[j], z_r.at[j, s], d_zu if up else d_zd)

    def y1(j, s, plus):
        ref = lg.at[j, y * ZL + s]
        return rcopy(ref, ref, y_s.at[j], y1_r.at[j, plus], d_yp if plus else d_ym)

    def y1_in(j, plus):
        ref = lg.at[j, pl.ds((ym if plus else yp) * ZL, ZL)]
        return rcopy(ref, ref, y_s.at[j], y1_r.at[j, plus], d_yp if plus else d_ym)

    def y2(j, plus):
        b = ym * ZL if plus else yp * ZL + ZL // 2
        ref = lg.at[j, pl.ds(b, ZL // 2)]
        return rcopy(ref, ref, y_s.at[j], y2_r.at[j], d_yp if plus else d_ym)

    def y2_in(j):
        ref = lg.at[j, pl.ds(((y + 2) % 4) * ZL, ZL)]
        return rcopy(ref, ref, y_s.at[j], y2_r.at[j], d_yp)

    def rs1(j, plus):
        if plus:
            return rcopy(part.at[j, xo, 0], rh.at[j, 1], rs_s.at[j], rs1_r.at[j, 1], d_xp)
        return rcopy(part.at[j, xo, 1], rh.at[j, 0], rs_s.at[j], rs1_r.at[j, 0], d_xm)

    def rs2(j, plus):
        if plus:
            return rcopy(part.at[j, xp], rf.at[j, 1], rs_s.at[j], rs2_r.at[j], d_xp)
        return rcopy(part.at[j, xm], rf.at[j, 0], rs_s.at[j], rs2_r.at[j], d_xm)

    def rs2_in(j):
        return rcopy(rf.at[j], rf.at[j], rs_s.at[j], rs2_r.at[j], d_xp)

    def z4(j):
        return rcopy(part.at[j, x], zr.at[j], z4_s.at[j], z4_r.at[j], d_z4)

    def ag1(j, plus):
        ref = out.at[x, :, c, j]
        return rcopy(ref, ref, ag_s.at[j], ag1_r.at[j, plus], d_xp if plus else d_xm)

    def ag2(j, plus):
        ref = out.at[xm, 0, c, j] if plus else out.at[xp, 1, c, j]
        return rcopy(ref, ref, ag_s.at[j], ag2_r.at[j], d_xp if plus else d_xm)

    def ag2_in(j):
        ref = out.at[xo, :, c, j]
        return rcopy(ref, ref, ag_s.at[j], ag2_r.at[j], d_xp)

    def core(j, k):
        ref = out.at[(x + k) % 4, :, c, j]
        return rcopy(ref, ref, core_s.at[j], core_r.at[j], d_c)

    def core_all(j):
        ref = out.at[:, :, c, j]
        return rcopy(ref, ref, core_s.at[j], core_r.at[j], d_c)

    def drain_left(j):
        sent = lg.at[j, pl.ds(0, 3 * ZL)]
        rcopy(sent, sent, y_s.at[j], y2_r.at[j], d_yp).wait_send()
        line = j >= DIRECT
        edge = jnp.logical_or(zl == 0, zl == ZL - 1)
        inner = jnp.logical_not(edge)
        for n, here in ((3, j < DIRECT), (1, jnp.logical_and(line, edge)), (5, jnp.logical_and(line, inner))):

            @pl.when(here)
            def _():
                some = lg.at[j, pl.ds(0, n)]
                rcopy(some, some, z_s.at[j], z_r.at[j, 0], d_c).wait_send()

    def drain_sums(j):
        sent = part.at[j, pl.ds(0, 3)]
        rcopy(sent, sent, rs_s.at[j], rs2_r.at[j], d_xp).wait_send()

    def drain_out(j):
        sent = out.at[pl.ds(0, 3), :, c, j]
        rcopy(sent, sent, ag_s.at[j], ag2_r.at[j], d_xp).wait_send()
        z4(j).wait_send()
        sent = out.at[:, :, c, j]
        rcopy(sent, sent, core_s.at[j], core_r.at[j], d_c).wait_send()
        came = out.at[:, :, 1 - c, j]
        rcopy(came, came, core_s.at[j], core_r.at[j], d_c).wait_recv()

    def st_own_z(j):
        @pl.when(j < DIRECT)
        def _():
            for q in range(ZL):
                pl.when(zl != q)(lambda: z_direct(j, q).start())

        @pl.when(j >= DIRECT)
        def _():
            pl.when(zl < ZL - 1)(lambda: z_own(j, 1).start())
            pl.when(zl > 0)(lambda: z_own(j, 0).start())

    def st_own_y(j):
        y1(j, zl, 1).start()
        y1(j, zl, 0).start()

    def st_z(k, j):
        for up in (1, 0):
            s = zl - k if up else zl + k
            there = (s >= 0) if up else (s < ZL)
            on = jnp.logical_and(j >= DIRECT, (zl < ZL - 1) if up else (zl > 0))

            @pl.when(there)
            def _():
                z_fwd(j, s, up).wait_recv()

                @pl.when(on)
                def _():
                    z_fwd(j, s, up).start()

    def st_y1(j):
        for k in range(1, ZL):
            s = (zl + k) % ZL
            y1(j, s, 1).start()
            y1(j, s, 0).start()

    def st_y2(j):
        y1_in(j, 1).wait_recv()
        y2(j, 1).start()
        y1_in(j, 0).wait_recv()
        y2(j, 0).start()

    def st_gemm(j):
        @pl.when(j == 0)
        def _():
            r_loc.wait()
            w_loc.wait()
            r_rem.wait_recv()

        y2_in(j).wait_recv()
        lhs = jnp.concatenate([lg[j, s] for s in range(TP)], axis=1)
        for n in range(4):
            rhs = rall[:, :, :, 256 * n : 256 * n + 256].reshape(TP * 2 * n_mem, 256)
            acc = jnp.dot(lhs, rhs, preferred_element_type=F32)
            part[j, :, :, :, 256 * n : 256 * n + 256] = acc.astype(BF16).reshape(X, ZH, DR, 256)
        rs1(j, 1).start()
        rs1(j, 0).start()

    def st_rs2(j):
        rs1(j, 1).wait_recv()
        part[j, xp, 0] = (part[j, xp, 0].astype(F32) + rh[j, 1].astype(F32)).astype(BF16)
        rs2(j, 1).start()
        rs1(j, 0).wait_recv()
        part[j, xm, 1] = (part[j, xm, 1].astype(F32) + rh[j, 0].astype(F32)).astype(BF16)
        rs2(j, 0).start()

    def st_sum(j):
        rs2_in(j).wait_recv()
        w = wv[j].astype(F32)
        for h in range(ZH):
            mine = part[j, x, h].astype(F32) + jnp.where(zh == h, w, 0.0)
            part[j, x, h] = (mine + rf[j, 1, h].astype(F32) + rf[j, 0, h].astype(F32)).astype(BF16)
        z4(j).start()
        drain_left(j)

    def st_fin(j):
        z4(j).wait_recv()
        for h in range(ZH):
            out[x, h, c, j] = (part[j, x, h].astype(F32) + zr[j, h].astype(F32)).astype(BF16)
        ag1(j, 1).start()
        ag1(j, 0).start()
        pl.when(j >= J - 2)(lambda: core(j, 0).start())
        drain_sums(j)

    def st_ag2(j):
        ag1(j, 1).wait_recv()
        ag2(j, 1).start()
        ag1(j, 0).wait_recv()
        ag2(j, 0).start()

        @pl.when(j >= J - 2)
        def _():
            core(j, 3).start()
            core(j, 1).start()

    def st_last(j):
        @pl.when(j == 0)
        def _():
            m_rem.wait_send()
            ranks_rem.wait_send()
            r_rem.wait_send()

        ag2_in(j).wait_recv()
        pl.when(j >= J - 2)(lambda: core(j, 2).start())
        pl.when(j < J - 2)(lambda: core_all(j).start())
        pl.when(j >= 2)(lambda: drain_out(j - 2))

    stages = (
        st_own_z,
        st_own_y,
        functools.partial(st_z, 1),
        functools.partial(st_z, 2),
        functools.partial(st_z, 3),
        st_y1,
        st_y2,
        st_gemm,
        st_rs2,
        st_sum,
        st_fin,
        st_ag2,
        st_last,
    )

    def step(i, carry):
        word, counts = carry[0], carry[1:]
        now = lax.rem(word, 16)
        for n, fn in enumerate(stages):

            @pl.when(now == n)
            def _():
                fn(counts[n])

        return (lax.div(word, 16),) + tuple(
            jnp.where(now == n, count + 1, count) for n, count in enumerate(counts)
        )

    def group(g, counts):
        word = jnp.int32(ORDER[0])
        for k, w in enumerate(ORDER):
            word = jnp.where(g == k, jnp.int32(w), word)
        return lax.fori_loop(0, STEPS, step, (word,) + counts)[1:]

    lax.fori_loop(0, len(ORDER), group, (jnp.int32(0),) * len(stages))
    drain_out(J - 2)
    drain_out(J - 1)


def per_device(left_factors, right_factors, ranks, weight):
    n_mem, width = left_factors.shape
    members, cols = right_factors.shape
    total = members * lax.axis_size("pop")
    J = CHUNKS
    DR = weight.shape[0] // J
    dma = pltpu.SemaphoreType.DMA
    anyspace = pl.BlockSpec(memory_space=pl.ANY)
    vmem = pl.BlockSpec(memory_space=pltpu.VMEM)
    out = pl.pallas_call(
        functools.partial(kernel, total),
        out_shape=pltpu.VMEM((X, ZH, CORES, J, DR, cols), BF16),
        in_specs=[anyspace] * 4,
        out_specs=vmem,
        scratch_shapes=[
            pltpu.VMEM((2, 1, n_mem), jnp.int32),
            pltpu.VMEM((2, n_mem, width // 2), BF16),
            pltpu.VMEM((J, TP, 8 * DR, 2 * n_mem), BF16),
            pltpu.VMEM((TP, 2, n_mem, cols), BF16),
            pltpu.VMEM((J, DR, cols), BF16),
            pltpu.VMEM((J, X, ZH, DR, cols), BF16),
            pltpu.VMEM((J, 2, DR, cols), BF16),
            pltpu.VMEM((J, 2, ZH, DR, cols), BF16),
            pltpu.VMEM((J, ZH, DR, cols), BF16),
            dma((10,)),
            dma((J,)),
            dma((J, ZL)),
            dma((J,)),
            dma((J, 2)),
            dma((J,)),
            dma((J,)),
            dma((J, 2)),
            dma((J,)),
            dma((J,)),
            dma((J,)),
            dma((J,)),
            dma((J, 2)),
            dma((J,)),
            dma((J,)),
            dma((J,)),
        ],
        compiler_params=pltpu.CompilerParams(
            collective_id=0, has_side_effects=True, vmem_limit_bytes=48 * 2**20
        ),
    )(
        left_factors,
        ranks.reshape(1, n_mem),
        right_factors.reshape(TP, n_mem, cols),
        weight.reshape(J, DR, cols),
    )
    return out.reshape(X * ZH * CORES * J * DR, cols)


def solution(mesh):
    return jax.shard_map(
        per_device,
        mesh=mesh,
        in_specs=(P(("pop", "tp"), None), P("pop", "tp"), P(("pop", "tp")), P("pop", "tp")),
        out_specs=P(None, "tp"),
        check_vma=False,
    )
```
